32 devices in a mesh: seq: 8 (over z, x), head: 4 (over y, core).
Axes of the slice: x: 2, y: 2, z: 4, core: 2. Of those that a mesh axis runs over, the one named last changes fastest.
Arguments:
- queries: bfloat16 [4096, 2048], P('seq', 'head'), may hold values from -6 to 6
- keys: bfloat16 [4096, 2048], P('seq', 'head'), may hold values from -6 to 6
- values: bfloat16 [4096, 2048], P('seq', 'head'), may hold values from -6 to 6
- summary_lists: int32 [8, 8, 16], P('seq', 'head'), may hold values from 0 to 6, as said below
- out_weight: bfloat16 [2048, 2048], P('head'), may hold values from -0.125 to 0.125
Outputs:
- mixed: bfloat16 [4096, 2048], P(('seq', 'head'))
The draws below stay inside these ranges and needn't reach their ends.
Inputs may be any that keep to these rules, and one draw needn't show every extreme that they name: `summary_lists`: entry [b, f, k] names a block. In every query block b above 0 it is below b, and entry [b, f, 0] is b - 1; in query block 0 every entry is 0 and names nothing. Entries may repeat.
All inputs are finite; a program needn't handle non-finite values.
Results may differ from the reference program's by a relative error of at most 0.014.
Values may be sent and summed in bfloat16 or wider, within the bound.
No kernel may reach another device: no remote copies, remote signals or barrier semaphores. Data moves between devices by JAX's collectives and lax.ppermute only.
A program may use at most 64 MiB of HBM per device.

```python
import jax
import jax.numpy as jnp
from jax import lax

HEADS = 16
HEAD_DIM = 128
BLK = 512
SUMMARY = 32
PICKS = 16
D = 2048
NBLK = 8
TOKENS = 4096


def draw_queries(key, part):
    noise_key = jax.random.fold_in(key, 11)
    field = jnp.clip(1.2 * jax.random.normal(noise_key, (TOKENS, D), jnp.float32), -6.0, 6.0)
    return field.astype(jnp.bfloat16)


def draw_keys(key, part):
    noise_key = jax.random.fold_in(key, 13)
    field = jnp.clip(1.2 * jax.random.normal(noise_key, (TOKENS, D), jnp.float32), -6.0, 6.0)
    return field.astype(jnp.bfloat16)


def draw_summary_lists(key, part):
    block = jnp.arange(NBLK, dtype=jnp.int32)[:, None, None]
    upper = jnp.maximum(block, 1)
    picked = jax.random.randint(key, (NBLK, HEADS // 2, PICKS), 0, upper, dtype=jnp.int32)
    before = jnp.broadcast_to(jnp.maximum(block - 1, 0), (NBLK, HEADS // 2, 1))
    return jnp.concatenate([before, picked[:, :, 1:]], axis=2).astype(jnp.int32)


def block_scale(own_key, dims, cuts, least, top_value):
    level = 1.0
    for axis_at, parts in cuts:
        draws = jax.random.uniform(jax.random.fold_in(jax.random.fold_in(own_key, 6), axis_at), (parts,), jnp.float32, least / len(cuts), top_value / len(cuts))
        level = level * jnp.repeat(jnp.exp(draws), dims[axis_at] // parts).reshape((-1,) + (1,) * (len(dims) - 1 - axis_at))
    return level


def gaussian(stream_key, extent, width, bound, cuts=(), kind=jnp.bfloat16):
    values = width * jax.random.normal(stream_key, extent, jnp.float32)
    if cuts:
        values = values * block_scale(stream_key, extent, cuts, -0.22, 0.18)
    return jnp.clip(values, -bound, bound).astype(kind)


def setup_inputs(seed: int = 0) -> dict:
    arg_keys = jax.random.split(jax.random.key(seed), 6)
    queries = draw_queries(jax.random.fold_in(arg_keys[5], 71), 0)
    keys = draw_keys(jax.random.fold_in(arg_keys[5], 71), 0)
    values = gaussian(arg_keys[2], (TOKENS, D), 1.5, 6.0, ((0, 8), (1, 4)))
    summary_lists = draw_summary_lists(jax.random.fold_in(arg_keys[5], 71), 0)
    out_weight = gaussian(arg_keys[4], (D, D), D ** -0.5, 0.125, ((0, 4),))
    return {"queries": queries, "keys": keys, "values": values, "summary_lists": summary_lists, "out_weight": out_weight}


NEG = -1e30


def masked_softmax(scores, valid):
    scores = jnp.where(valid, scores, NEG)
    peak = jnp.max(scores, axis=-1, keepdims=True)
    weights = jnp.where(valid, jnp.exp(scores - peak), 0.0)
    return weights / jnp.sum(weights, axis=-1, keepdims=True)


def row_head(head_q, head_k, head_v):
    scale = HEAD_DIM ** -0.5
    causal = jnp.arange(BLK)[:, None] >= jnp.arange(BLK)[None, :]

    def one_block(block):
        block_q, block_k, block_v = block
        scores = jnp.dot(block_q, block_k.T, preferred_element_type=jnp.float32) * scale
        weights = masked_softmax(scores, causal).astype(jnp.bfloat16)
        return jnp.dot(weights, block_v, preferred_element_type=jnp.float32).astype(jnp.bfloat16)

    return lax.map(one_block, (head_q, head_k, head_v))


def column_head(head_q, head_k, head_v):
    scale = HEAD_DIM ** -0.5
    col_q = jnp.swapaxes(head_q, 0, 1).astype(jnp.float32)
    col_k = jnp.swapaxes(head_k, 0, 1).astype(jnp.float32)
    col_v = jnp.swapaxes(head_v, 0, 1).astype(jnp.float32)
    scores = jnp.einsum('crd,csd->crs', col_q, col_k) * scale
    earlier = jnp.arange(NBLK)[:, None] >= jnp.arange(NBLK)[None, :]
    weights = masked_softmax(scores, earlier[None]).astype(jnp.bfloat16)
    result = jnp.einsum('crs,csd->crd', weights.astype(jnp.float32), col_v)
    return jnp.swapaxes(result, 0, 1).astype(jnp.bfloat16)


def fixed_head(head_q, head_k, head_v, lists):
    scale = HEAD_DIM ** -0.5
    causal = jnp.arange(BLK)[:, None] >= jnp.arange(BLK)[None, :]
    tail_k = head_k[:, BLK - SUMMARY:, :]
    tail_v = head_v[:, BLK - SUMMARY:, :]

    def one_block(item):
        block_q, block_k, block_v, picks, index = item
        own_scores = jnp.dot(block_q, block_k.T, preferred_element_type=jnp.float32) * scale
        far_k = tail_k[picks].reshape(PICKS * SUMMARY, HEAD_DIM)
        far_v = tail_v[picks].reshape(PICKS * SUMMARY, HEAD_DIM)
        far_scores = jnp.dot(block_q, far_k.T, preferred_element_type=jnp.float32) * scale
        usable = jnp.repeat(picks < index, SUMMARY)
        scores = jnp.concatenate([own_scores, far_scores], axis=1)
        valid = jnp.concatenate([causal, jnp.broadcast_to(usable[None, :], (BLK, PICKS * SUMMARY))], axis=1)
        weights = masked_softmax(scores, valid).astype(jnp.bfloat16)
        stacked = jnp.concatenate([block_v, far_v], axis=0)
        return jnp.dot(weights, stacked, preferred_element_type=jnp.float32).astype(jnp.bfloat16)

    return lax.map(one_block, (head_q, head_k, head_v, lists, jnp.arange(NBLK, dtype=jnp.int32)))


def reference(queries, keys, values, summary_lists, out_weight):
    def head_part(source, head):
        return source[:, head * HEAD_DIM:(head + 1) * HEAD_DIM].reshape(NBLK, BLK, HEAD_DIM)

    pieces = []
    for head in range(HEADS):
        head_q = head_part(queries, head)
        head_k = head_part(keys, head)
        head_v = head_part(values, head)
        kind = head % 4
        if kind == 0:
            result = row_head(head_q, head_k, head_v)
        elif kind == 1:
            result = column_head(head_q, head_k, head_v)
        else:
            result = fixed_head(head_q, head_k, head_v, summary_lists[:, 2 * (head // 4) + kind - 2, :])
        pieces.append(result.reshape(TOKENS, HEAD_DIM))
    attended = jnp.concatenate(pieces, axis=1)
    return jnp.dot(attended, out_weight, preferred_element_type=jnp.float32).astype(jnp.bfloat16)
```

```python
import functools
import math

import jax
import jax.numpy as jnp
from jax import lax
from jax.experimental import pallas as pl
from jax.experimental.pallas import tpu as pltpu
from jax.sharding import PartitionSpec as P

HEAD_DIM = 128
SUMMARY = 32
NEG = -1e30
BF16 = jnp.bfloat16
F32 = jnp.float32
VMEM = pl.BlockSpec(memory_space=pltpu.VMEM)
SCALE2 = HEAD_DIM ** (-0.5) * math.log2(math.e)


def call(kernel, out, operands, flops=0):
    out = [jax.ShapeDtypeStruct(shape, BF16) for shape in out]
    moved = sum(x.size * x.dtype.itemsize for x in operands) + sum(2 * math.prod(x.shape) for x in out)
    return pl.pallas_call(
        kernel,
        out_shape=out,
        in_specs=[VMEM] * len(operands),
        out_specs=[VMEM] * len(out),
        compiler_params=pltpu.CompilerParams(vmem_limit_bytes=40 * 1024 * 1024),
        cost_estimate=pl.CostEstimate(flops=flops, bytes_accessed=moved, transcendentals=flops // 512),
    )(*operands)


def dot_t(a, b):
    return lax.dot_general(a, b, (((1,), (1,)), ((), ())), preferred_element_type=F32)


def dot(a, b):
    return jnp.dot(a, b, preferred_element_type=F32)


def masked_attention(q, k, v, valid):
    scores = jnp.where(valid, dot_t(q, k), NEG)
    peak = jnp.max(scores, axis=1, keepdims=True)
    weights = jnp.exp2((scores - peak) * SCALE2)
    denom = jnp.sum(weights, axis=1, keepdims=True)
    return dot(weights.astype(BF16), v) / denom


def column_kernel(columns, moved_ref, out_ref):
    outer, _, inner, depth = moved_ref.shape
    rows = outer * inner
    q, k, v = (moved_ref[:, i].reshape(rows, depth) for i in range(3))
    at_q = lax.broadcasted_iota(jnp.int32, (rows, 1), 0)
    at_k = lax.broadcasted_iota(jnp.int32, (1, rows), 1)
    valid = (lax.rem(at_q, columns) == lax.rem(at_k, columns)) & (at_k <= at_q)
    out = masked_attention(q, k, v, valid)
    out_ref[...] = out.astype(BF16).reshape(outer, inner, depth)


def part_kernel(flips, parts, stages, q_ref, k_ref, v_ref, w_ref, mult_ref, *refs):
    tails, outs = refs[:stages], refs[stages:]
    block = q_ref.shape[0]
    rows = block // parts
    me = lax.axis_index("head")
    far = [[], [], [], []]
    for tail in tails:
        for slot in range(tail.shape[0]):
            for i in range(4):
                far[i].append(tail[slot, i])
    far = [jnp.concatenate(x, axis=0) for x in far]
    for flip, out_ref in zip(flips, outs):
        first = pl.multiple_of((me ^ flip) * rows, rows)
        at_q = first + lax.broadcasted_iota(jnp.int32, (rows, 1), 0)
        at_k = lax.broadcasted_iota(jnp.int32, (1, block), 1)
        causal = at_k <= at_q
        q = q_ref[pl.ds(first, rows), :]
        attended = masked_attention(q[:, :HEAD_DIM], k_ref[:, :HEAD_DIM], v_ref[:, :HEAD_DIM], causal)
        total = dot(attended.astype(BF16), w_ref[:HEAD_DIM])
        for f in range(2):
            cols = slice((2 + f) * HEAD_DIM, (3 + f) * HEAD_DIM)
            mult = mult_ref[f : f + 1, :]
            own = jnp.where(causal, dot_t(q[:, cols], k_ref[:, cols]), NEG)
            away = jnp.where(mult > 0, dot_t(q[:, cols], far[f]), NEG)
            peak = jnp.maximum(jnp.max(own, axis=1, keepdims=True), jnp.max(away, axis=1, keepdims=True))
            own = jnp.exp2((own - peak) * SCALE2)
            away = jnp.exp2((away - peak) * SCALE2) * mult
            denom = jnp.sum(own, axis=1, keepdims=True) + jnp.sum(away, axis=1, keepdims=True)
            attended = (dot(own.astype(BF16), v_ref[:, cols]) + dot(away.astype(BF16), far[2 + f])) / denom
            total += dot(attended.astype(BF16), w_ref[cols, :])
        out_ref[...] = total.astype(BF16)


def last_kernel(own_ref, core_ref, far_ref, moved_ref, w0, w1, w2, w3, out_ref):
    total = own_ref[...].astype(F32) + core_ref[...].astype(F32) + far_ref[...].astype(F32)
    outer, heads, inner, depth = moved_ref.shape
    for flip, w in enumerate((w0, w1, w2, w3)):
        total += dot(moved_ref[:, flip].reshape(outer * inner, depth), w[...])
    out_ref[...] = total.astype(BF16)


def swap(x, axis, flip, count):
    return lax.ppermute(x, axis, [(i, i ^ flip) for i in range(count)])


def gather_tails(mine, count):
    have, arrays = 1, [mine[None]]
    while have < count:
        held = arrays[0] if len(arrays) == 1 else jnp.concatenate(arrays, axis=0)
        radix = 2 if have == 1 or count == 2 * have else 4
        arrays = [held] + [swap(held, "seq", have * i, count) for i in range(1, radix)]
        have *= radix
    return arrays


def per_device(queries, keys, values, summary_lists, out_weight):
    count, parts = lax.axis_size("seq"), lax.axis_size("head")
    block = queries.shape[0]
    me = lax.axis_index("seq")
    per = block // (count * parts)
    columns = per * parts
    col = slice(HEAD_DIM, 2 * HEAD_DIM)

    tail = jnp.stack(
        [x[block - SUMMARY :, h * HEAD_DIM : (h + 1) * HEAD_DIM] for x in (keys, values) for h in (2, 3)]
    )
    tails = gather_tails(tail, count)

    packed = jnp.stack([x[:, col].reshape(parts, count, per, HEAD_DIM) for x in (queries, keys, values)])
    packed = packed.transpose(2, 0, 1, 3, 4).reshape(count, 3 * columns, HEAD_DIM)
    moved = lax.all_to_all(packed, "seq", split_axis=0, concat_axis=0, tiled=True)
    moved = moved.reshape(count, 3, columns, HEAD_DIM)
    if columns % 16:
        moved = moved.transpose(1, 0, 2, 3).reshape(1, 3, block, HEAD_DIM)

    w_col = out_weight[col]
    w_far = swap(w_col, "head", 2, parts)
    w_core = swap(w_col, "head", 1, parts)
    w_both = swap(w_far, "head", 1, parts)

    slot_block = me ^ jnp.arange(count, dtype=jnp.int32)
    names = (summary_lists[0][:, :, None] == slot_block) & (slot_block < me)
    mult = jnp.repeat(jnp.sum(names.astype(F32), axis=1), SUMMARY, axis=1)

    def partial_sums(flips):
        shape = (block // parts, out_weight.shape[1])
        flops = len(flips) * shape[0] * 2 * 3 * HEAD_DIM * (3 * block + shape[1])
        return call(
            functools.partial(part_kernel, flips, parts, len(tails)),
            [shape] * len(flips),
            (queries, keys, values, out_weight, mult, *tails),
            flops,
        )

    (both_sum,) = partial_sums((3,))
    both_in = swap(both_sum, "head", 1, parts)
    (far_sum,) = partial_sums((2,))
    far_in = swap((far_sum.astype(F32) + both_in.astype(F32)).astype(BF16), "head", 2, parts)
    core_sum, own_sum = partial_sums((1, 0))
    core_in = swap(core_sum, "head", 1, parts)

    column_shape = (moved.shape[0], moved.shape[2], HEAD_DIM)
    (column_out,) = call(
        functools.partial(column_kernel, columns), [column_shape], (moved,), 4 * block * block * HEAD_DIM
    )
    column_out = column_out.reshape(count * parts, per, HEAD_DIM)
    back = lax.all_to_all(column_out, ("seq", "head"), split_axis=0, concat_axis=0, tiled=True)
    back = back.reshape(count, parts, per, HEAD_DIM)
    if per % 16:
        back = back.transpose(1, 0, 2, 3).reshape(1, parts, count * per, HEAD_DIM)
    back = back[:, lax.axis_index("head") ^ jnp.arange(parts)]
    (mixed,) = call(
        last_kernel,
        [own_sum.shape],
        (own_sum, core_in, far_in, back, w_col, w_core, w_far, w_both),
        2 * own_sum.size * parts * HEAD_DIM,
    )
    return mixed


def solution(mesh):
    return jax.shard_map(
        per_device,
        mesh=mesh,
        in_specs=(
            P("seq", "head"),
            P("seq", "head"),
            P("seq", "head"),
            P("seq", "head", None),
            P("head", None),
        ),
        out_specs=P(("seq", "head"), None),
        check_vma=False,
    )
```

```python
import functools
import math

import jax
import jax.numpy as jnp
from jax import lax
from jax.experimental import pallas as pl
from jax.experimental.pallas import tpu as pltpu
from jax.sharding import PartitionSpec as P

HEAD_DIM = 128
SUMMARY = 32
NEG = -1e30
JOIN_COST = 10**10
LAST_COST = 10**10
OWN_ROOM = 48
BF16 = jnp.bfloat16
F32 = jnp.float32
HBM = pl.BlockSpec(memory_space=pltpu.HBM)
VMEM = pl.BlockSpec(memory_space=pltpu.VMEM)
SCALE2 = HEAD_DIM ** (-0.5) * math.log2(math.e)


def call(kernel, out, operands, scratch=(), copies=1, cost=1, room=24):
    return pl.pallas_call(
        kernel,
        out_shape=[jax.ShapeDtypeStruct(x[1], x[2] if len(x) > 2 else BF16) for x in out],
        in_specs=[memory for memory, _ in operands],
        out_specs=[x[0] for x in out],
        scratch_shapes=[*scratch, pltpu.SemaphoreType.DMA((copies,))],
        compiler_params=pltpu.CompilerParams(vmem_limit_bytes=room * 2**20),
        cost_estimate=pl.CostEstimate(flops=cost, bytes_accessed=1, transcendentals=0),
    )(*(x for _, x in operands))


def start(sems, pairs, first=0):
    copies = [pltpu.make_async_copy(src, dst, sems.at[first + i]) for i, (src, dst) in enumerate(pairs)]
    for copy in copies:
        copy.start()
    return copies


def wait(copies):
    for copy in copies:
        copy.wait()


def dot_t(a, b):
    return lax.dot_general(a, b, (((1,), (1,)), ((), ())), preferred_element_type=F32)


def dot(a, b):
    return jnp.dot(a, b, preferred_element_type=F32)


def weigh(scores, valid):
    scores = jnp.where(valid, scores, NEG)
    peak = jnp.max(scores, axis=1, keepdims=True)
    weights = jnp.exp2((scores - peak) * SCALE2)
    return weights.astype(BF16), jnp.sum(weights, axis=1, keepdims=True), peak


def head(h):
    return slice(h * HEAD_DIM, (h + 1) * HEAD_DIM)


def tail_kernel(k_ref, v_ref, tail, sems):
    block = k_ref.shape[0]
    pairs = []
    for i, ref in enumerate((k_ref, v_ref)):
        for f in range(2):
            pairs.append((ref.at[pl.ds(block - SUMMARY, SUMMARY), pl.ds((2 + f) * HEAD_DIM, HEAD_DIM)], tail.at[2 * i + f]))
    wait(start(sems, pairs))


def pack_kernel(q_ref, k_ref, v_ref, w_ref, packed_ref, w_col_ref, cols, w_col, sems):
    parts = q_ref.shape[0]
    come, leave = [], []
    for i, ref in enumerate((q_ref, k_ref, v_ref)):
        come.append((ref.at[:, :, :, pl.ds(HEAD_DIM, HEAD_DIM)], cols.at[i]))
        for part in range(parts):
            leave.append((cols.at[i, part], packed_ref.at[:, i, part]))
    come.append((w_ref.at[pl.ds(HEAD_DIM, HEAD_DIM)], w_col))
    leave.append((w_col, w_col_ref))
    come = start(sems, come)
    gone = []
    first = len(come)
    for copy, makes in zip(come, (parts, parts, parts, 1)):
        wait([copy])
        gone += start(sems, leave[:makes], first)
        leave, first = leave[makes:], first + makes
    wait(gone)


def pack(queries, keys, values, out_weight, count, parts, per):
    width = queries.shape[1]
    (tail,) = call(tail_kernel, [(VMEM, (4, SUMMARY, HEAD_DIM))], [(HBM, keys), (HBM, values)], (), 4, room=63)
    if per % 16:
        cut = [x[:, HEAD_DIM : 2 * HEAD_DIM].reshape(parts, count, per, HEAD_DIM) for x in (queries, keys, values)]
        packed = jnp.stack(cut).transpose(2, 0, 1, 3, 4)
        return packed, tail, out_weight[HEAD_DIM : 2 * HEAD_DIM]
    w_shape = (HEAD_DIM, out_weight.shape[1])
    cut = [x.reshape(parts, count, per, width) for x in (queries, keys, values)]
    packed, w_col = call(
        pack_kernel,
        [(HBM, (count, 3, parts, per, HEAD_DIM)), (HBM, w_shape)],
        [(HBM, x) for x in (*cut, out_weight)],
        [pltpu.VMEM((3, parts, count, per, HEAD_DIM), BF16), pltpu.VMEM(w_shape, BF16)],
        5 + 3 * parts,
        room=63,
    )
    return packed, tail, w_col


def column_kernel(columns, moved_ref, out_ref, held, done, sems):
    outer, _, inner, depth = moved_ref.shape
    rows = outer * inner
    copies = start(sems, [(moved_ref.at[:, i], held.at[i]) for i in range(3)])
    wait(copies[:2])
    q, k, v = (held.at[i] for i in range(3))
    step = HEAD_DIM
    results = []
    for first in range(0, rows, step):
        upto = first + step
        at_q = first + lax.broadcasted_iota(jnp.int32, (step, 1), 0)
        at_k = lax.broadcasted_iota(jnp.int32, (1, upto), 1)
        valid = (lax.rem(at_q, columns) == lax.rem(at_k, columns)) & (at_k <= at_q)
        q_rows = q[...].reshape(rows, depth)[first:upto]
        results.append((upto, *weigh(dot_t(q_rows, k[...].reshape(rows, depth)[:upto]), valid)))
    wait(copies[2:])
    out = [dot(weights, v[...].reshape(rows, depth)[:upto]) / denom for upto, weights, denom, _ in results]
    done[...] = jnp.concatenate(out, axis=0).astype(BF16).reshape(outer, inner, depth)
    wait(start(sems, [(done, out_ref)]))


def own_kernel(q_ref, k_ref, v_ref, w_ref, row_ref, sum_ref, stat_ref, q_fixed, w_all, q_all, k_all, v_all, sems):
    pairs = [(q_ref, q_all), (k_ref, k_all), (v_ref, v_all)]
    pairs += [(q_ref.at[:, pl.ds(2 * HEAD_DIM, 2 * HEAD_DIM)], q_fixed)]
    pairs += [(w_ref.at[pl.ds(0, HEAD_DIM)], w_all.at[pl.ds(0, HEAD_DIM)])]
    pairs += [(w_ref.at[pl.ds(2 * HEAD_DIM, 2 * HEAD_DIM)], w_all.at[pl.ds(HEAD_DIM, 2 * HEAD_DIM)])]
    copies = start(sems, pairs)
    wait(copies[:3])
    block, step = q_ref.shape[0], HEAD_DIM
    for first in range(0, block, step):
        upto = first + step
        rows = slice(first, upto)
        at_q = first + lax.broadcasted_iota(jnp.int32, (step, 1), 0)
        at_k = lax.broadcasted_iota(jnp.int32, (1, upto), 1)
        for h in (0, 2, 3):
            weights, denom, peak = weigh(dot_t(q_all[rows, head(h)], k_all[:upto, head(h)]), at_k <= at_q)
            total = dot(weights, v_all[:upto, head(h)])
            if h == 0:
                row_ref[rows] = (total / denom).astype(BF16)
            else:
                sum_ref[h - 2, rows] = total
                low = lax.broadcasted_iota(jnp.int32, (step, HEAD_DIM), 1) < HEAD_DIM // 2
                stat_ref[h - 2, rows] = jnp.where(low, denom, peak)
    wait(copies[3:])


def own_part(queries, keys, values, out_weight):
    block = queries.shape[0]
    state = (VMEM, (2, block, HEAD_DIM), F32)
    weight_shape = (3 * HEAD_DIM, out_weight.shape[1])
    return call(
        own_kernel,
        [(VMEM, (block, HEAD_DIM)), state, state, (VMEM, (block, 2 * HEAD_DIM)), (VMEM, weight_shape)],
        [(HBM, x) for x in (queries, keys, values, out_weight)],
        [pltpu.VMEM(queries.shape, BF16)] * 3,
        6,
        room=OWN_ROOM,
    )


def part_kernel(flips, parts, slots, row_ref, sum_ref, stat_ref, q_ref, w_ref, mult_ref, *refs):
    tails, refs = refs[: len(slots)], refs[len(slots) :]
    outs, (far, sems) = refs[: len(flips)], refs[len(flips) :]
    pairs, at = [], 0
    for tail, many in zip(tails, slots):
        pairs.append((tail, far.at[pl.ds(at, many)]))
        at += many
    wait(start(sems, pairs))
    rows = q_ref.shape[0] // parts
    me = lax.axis_index("head")
    away_kv = [far[:, i].reshape(at * SUMMARY, HEAD_DIM) for i in range(4)]
    for flip, out_ref in zip(flips, outs):
        here = pl.ds(pl.multiple_of((me ^ flip) * rows, rows), rows)
        found = [row_ref[here, :]]
        for f in range(2):
            mult = mult_ref[f : f + 1, :]
            away = jnp.where(mult > 0, dot_t(q_ref[here, head(f)], away_kv[f]), NEG)
            own_denom, own_peak = stat_ref[f, here, :1], stat_ref[f, here, HEAD_DIM // 2 : HEAD_DIM // 2 + 1]
            peak = jnp.maximum(own_peak, jnp.max(away, axis=1, keepdims=True))
            shrink = jnp.exp2((own_peak - peak) * SCALE2)
            away = jnp.exp2((away - peak) * SCALE2) * mult
            denom = own_denom * shrink + jnp.sum(away, axis=1, keepdims=True)
            total = sum_ref[f, here, :] * shrink + dot(away.astype(BF16), away_kv[2 + f])
            found.append((total / denom).astype(BF16))
        out_ref[...] = dot(jnp.concatenate(found, axis=1), w_ref[...]).astype(BF16)


def add_kernel(a_ref, b_ref, out_ref, _):
    out_ref[...] = (a_ref[...].astype(F32) + b_ref[...].astype(F32)).astype(BF16)


def join_kernel(*refs):
    at = 0
    for ref in refs[:-2]:
        refs[-2][at : at + ref.shape[0]] = ref[...]
        at += ref.shape[0]


def near_kernel(own_ref, core_ref, moved_ref, *refs):
    ws, (out_ref, sums, moved, w_all, sems) = refs[:-5], refs[-5:]
    pairs = [(moved_ref, moved)] + [(w, w_all.at[i]) for i, w in enumerate(ws)]
    pairs += [(ref, sums.at[i]) for i, ref in enumerate((own_ref, core_ref))]
    wait(start(sems, pairs))
    outer, heads, inner, depth = moved.shape
    me = lax.axis_index("head")
    found = jnp.concatenate([moved[:, me ^ i].reshape(outer * inner, depth) for i in range(heads)], axis=1)
    total = dot(found, w_all[...].reshape(heads * depth, w_all.shape[2]))
    out_ref[...] = total + sums[0].astype(F32) + sums[1].astype(F32)


def last_kernel(near_ref, far_ref, out_ref, near, far, done, sems):
    pieces = sems.shape[0] // 3
    cut = done.shape[1] // pieces
    cols = [pl.ds(i * cut, cut) for i in range(pieces)]
    copies = start(sems, [(a.at[:, c], b.at[:, c]) for c in cols for a, b in ((near_ref, near), (far_ref, far))])
    sent = []
    for i, c in enumerate(cols):
        wait(copies[2 * i : 2 * i + 2])
        done[:, c] = (near[:, c] + far[:, c].astype(F32)).astype(BF16)
        sent += start(sems, [(done.at[:, c], out_ref.at[:, c])], 2 * pieces + i)
    wait(sent)


def swap(x, axis, flip, count):
    return lax.ppermute(x, axis, [(i, i ^ flip) for i in range(count)])


def gather_tails(mine, count):
    order, arrays = [0], [mine[None]]
    bits = [(count // 4**i, 4) for i in range(1, 8) if count % 4**i == 0 and count // 4**i >= 2] + [(1, 2)]
    if count & (count - 1) or bits[-2:][0][0] != 2:
        return [lax.all_gather(mine, "seq")], None
    for step, radix in bits:
        held = arrays[0]
        if len(arrays) > 1:
            shape = (sum(x.shape[0] for x in arrays), *mine.shape)
            (held,) = call(join_kernel, [(VMEM, shape)], [(VMEM, x) for x in arrays], cost=JOIN_COST)
        arrays = [held] + [swap(held, "seq", step * i, count) for i in range(1, radix)]
        order = [j ^ (step * i) for i in range(radix) for j in order]
    return arrays, order


def per_device(queries, keys, values, summary_lists, out_weight):
    count, parts = lax.axis_size("seq"), lax.axis_size("head")
    block = queries.shape[0]
    me = lax.axis_index("seq")
    per = block // (count * parts)
    columns = per * parts

    packed, tail, w_col = pack(queries, keys, values, out_weight, count, parts, per)
    tails, order = gather_tails(tail, count)

    moved = lax.all_to_all(
        packed.reshape(count, 3 * columns, HEAD_DIM), "seq", split_axis=0, concat_axis=0, tiled=True
    )
    moved = moved.reshape(count, 3, columns, HEAD_DIM)
    if columns % 16:
        moved = moved.transpose(1, 0, 2, 3).reshape(1, 3, block, HEAD_DIM)

    w_far = swap(w_col, "head", 2, parts)
    w_core = swap(w_col, "head", 1, parts)
    w_both = swap(w_far, "head", 1, parts)

    slot_block = jnp.arange(count, dtype=jnp.int32) if order is None else me ^ jnp.array(order, jnp.int32)
    names = (summary_lists[0][:, :, None] == slot_block) & (slot_block < me)
    mult = jnp.repeat(jnp.sum(names.astype(F32), axis=1), SUMMARY, axis=1)

    shape = (block // parts, out_weight.shape[1])
    held = [queries, keys, values, out_weight]
    if len(tails) > 1:
        *held, tails[0] = lax.optimization_barrier((*held, tails[0]))
    own = own_part(*held)

    column_shape = (moved.shape[0], moved.shape[2], HEAD_DIM)
    (column_out,) = call(
        functools.partial(column_kernel, columns),
        [(HBM, column_shape)],
        [(HBM, moved)],
        [pltpu.VMEM((3, *column_shape), BF16), pltpu.VMEM(column_shape, BF16)],
        3,
    )

    def partial_sums(flips):
        return call(
            functools.partial(part_kernel, flips, parts, [x.shape[0] for x in tails]),
            [(VMEM, shape)] * len(flips),
            [(VMEM, x) for x in (*own, mult)] + [(HBM, x) for x in tails],
            [pltpu.VMEM((count, 4, SUMMARY, HEAD_DIM), BF16)],
            len(tails),
        )

    both_sum, far_sum = partial_sums((3, 2))
    both_in = swap(both_sum, "head", 1, parts)
    (far_sum,) = call(add_kernel, [(VMEM, shape)], [(VMEM, far_sum), (VMEM, both_in)])
    far_in = swap(far_sum, "head", 2, parts)
    core_sum, own_sum = partial_sums((1, 0))
    core_in = swap(core_sum, "head", 1, parts)

    column_out = column_out.reshape(count * parts, per, HEAD_DIM)
    back = lax.all_to_all(column_out, ("seq", "head"), split_axis=0, concat_axis=0, tiled=True)
    back = back.reshape(count, parts, per, HEAD_DIM)
    if per % 16:
        back = back.transpose(1, 0, 2, 3).reshape(1, parts, count * per, HEAD_DIM)
    (near_sum,) = call(
        near_kernel,
        [(VMEM, shape, F32)],
        [(HBM, x) for x in (own_sum, core_in, back, w_col, w_core, w_far, w_both)],
        [
            pltpu.VMEM((2, *shape), BF16),
            pltpu.VMEM(back.shape, BF16),
            pltpu.VMEM((parts, HEAD_DIM, shape[1]), BF16),
        ],
        3 + parts,
        cost=LAST_COST,
    )
    (mixed,) = call(
        last_kernel,
        [(HBM, shape)],
        [(HBM, near_sum), (HBM, far_in)],
        [pltpu.VMEM(shape, F32), pltpu.VMEM(shape, BF16), pltpu.VMEM(shape, BF16)],
        3 * 4,
    )
    return mixed


def solution(mesh):
    return jax.shard_map(
        per_device,
        mesh=mesh,
        in_specs=(
            P("seq", "head"),
            P("seq", "head"),
            P("seq", "head"),
            P("seq", "head", None),
            P("head", None),
        ),
        out_specs=P(("seq", "head"), None),
        check_vma=False,
    )
```

```python
import functools
import math

import jax
import jax.numpy as jnp
from jax import lax
from jax.experimental import pallas as pl
from jax.experimental.pallas import tpu as pltpu
from jax.sharding import PartitionSpec as P

HEAD_DIM = 128
SUMMARY = 32
NEG = -1e30
JOIN_COST = 10**9
COLUMN_COST = 10**9*3
LAST_COST = 1
OWN_ROOM = 48
BF16 = jnp.bfloat16
F32 = jnp.float32
HBM = pl.BlockSpec(memory_space=pltpu.HBM)
VMEM = pl.BlockSpec(memory_space=pltpu.VMEM)
SCALE2 = HEAD_DIM ** (-0.5) * math.log2(math.e)


def call(kernel, out, operands, scratch=(), copies=1, cost=1, room=24):
    return pl.pallas_call(
        kernel,
        out_shape=[jax.ShapeDtypeStruct(x[1], x[2] if len(x) > 2 else BF16) for x in out],
        in_specs=[memory for memory, _ in operands],
        out_specs=[x[0] for x in out],
        scratch_shapes=[*scratch, pltpu.SemaphoreType.DMA((copies,))],
        compiler_params=pltpu.CompilerParams(vmem_limit_bytes=room * 2**20),
        cost_estimate=pl.CostEstimate(flops=cost, bytes_accessed=1, transcendentals=0),
    )(*(x for _, x in operands))


def start(sems, pairs, first=0):
    copies = [pltpu.make_async_copy(src, dst, sems.at[first + i]) for i, (src, dst) in enumerate(pairs)]
    for copy in copies:
        copy.start()
    return copies


def wait(copies):
    for copy in copies:
        copy.wait()


def dot_t(a, b):
    return lax.dot_general(a, b, (((1,), (1,)), ((), ())), preferred_element_type=F32)


def dot(a, b):
    return jnp.dot(a, b, preferred_element_type=F32)


def weigh(scores, valid):
    scores = jnp.where(valid, scores, NEG)
    peak = jnp.max(scores, axis=1, keepdims=True)
    weights = jnp.exp2((scores - peak) * SCALE2)
    return weights.astype(BF16), jnp.sum(weights, axis=1, keepdims=True), peak


def head(h):
    return slice(h * HEAD_DIM, (h + 1) * HEAD_DIM)


def tail_kernel(k_ref, v_ref, tail, sems):
    block = k_ref.shape[0]
    pairs = []
    for i, ref in enumerate((k_ref, v_ref)):
        for f in range(2):
            pairs.append((ref.at[pl.ds(block - SUMMARY, SUMMARY), pl.ds((2 + f) * HEAD_DIM, HEAD_DIM)], tail.at[2 * i + f]))
    wait(start(sems, pairs))


def pack_kernel(q_ref, k_ref, v_ref, w_ref, packed_ref, w_col_ref, cols, w_col, sems):
    parts = q_ref.shape[0]
    come, leave = [], []
    for i, ref in enumerate((q_ref, k_ref, v_ref)):
        come.append((ref.at[:, :, :, pl.ds(HEAD_DIM, HEAD_DIM)], cols.at[i]))
        for part in range(parts):
            leave.append((cols.at[i, part], packed_ref.at[:, i, part]))
    come.append((w_ref.at[pl.ds(HEAD_DIM, HEAD_DIM)], w_col))
    leave.append((w_col, w_col_ref))
    come = start(sems, come)
    gone = []
    first = len(come)
    for copy, makes in zip(come, (parts, parts, parts, 1)):
        wait([copy])
        gone += start(sems, leave[:makes], first)
        leave, first = leave[makes:], first + makes
    wait(gone)


def pack(queries, keys, values, out_weight, count, parts, per):
    width = queries.shape[1]
    (tail,) = call(tail_kernel, [(VMEM, (4, SUMMARY, HEAD_DIM))], [(HBM, keys), (HBM, values)], (), 4, room=63)
    if per % 16:
        cut = [x[:, HEAD_DIM : 2 * HEAD_DIM].reshape(parts, count, per, HEAD_DIM) for x in (queries, keys, values)]
        packed = jnp.stack(cut).transpose(2, 0, 1, 3, 4)
        return packed, tail, out_weight[HEAD_DIM : 2 * HEAD_DIM]
    w_shape = (HEAD_DIM, out_weight.shape[1])
    cut = [x.reshape(parts, count, per, width) for x in (queries, keys, values)]
    packed, w_col = call(
        pack_kernel,
        [(HBM, (count, 3, parts, per, HEAD_DIM)), (HBM, w_shape)],
        [(HBM, x) for x in (*cut, out_weight)],
        [pltpu.VMEM((3, parts, count, per, HEAD_DIM), BF16), pltpu.VMEM(w_shape, BF16)],
        5 + 3 * parts,
        room=63,
    )
    return packed, tail, w_col


def column_kernel(columns, moved_ref, out_ref, held, done, sems):
    outer, _, inner, depth = moved_ref.shape
    rows = outer * inner
    copies = start(sems, [(moved_ref.at[:, i], held.at[i]) for i in range(3)])
    wait(copies[:2])
    q, k, v = (held.at[i] for i in range(3))
    step = HEAD_DIM
    results = []
    for first in range(0, rows, step):
        upto = first + step
        at_q = first + lax.broadcasted_iota(jnp.int32, (step, 1), 0)
        at_k = lax.broadcasted_iota(jnp.int32, (1, upto), 1)
        valid = (lax.rem(at_q, columns) == lax.rem(at_k, columns)) & (at_k <= at_q)
        q_rows = q[...].reshape(rows, depth)[first:upto]
        results.append((upto, *weigh(dot_t(q_rows, k[...].reshape(rows, depth)[:upto]), valid)))
    wait(copies[2:])
    out = [dot(weights, v[...].reshape(rows, depth)[:upto]) / denom for upto, weights, denom, _ in results]
    done[...] = jnp.concatenate(out, axis=0).astype(BF16).reshape(outer, inner, depth)
    wait(start(sems, [(done, out_ref)]))


def own_kernel(q_ref, k_ref, v_ref, w_ref, row_ref, sum_ref, stat_ref, q_fixed, w_all, q_all, k_all, v_all, sems):
    pairs = [(q_ref, q_all), (k_ref, k_all), (v_ref, v_all)]
    pairs += [(q_ref.at[:, pl.ds(2 * HEAD_DIM, 2 * HEAD_DIM)], q_fixed)]
    pairs += [(w_ref.at[pl.ds(0, HEAD_DIM)], w_all.at[pl.ds(0, HEAD_DIM)])]
    pairs += [(w_ref.at[pl.ds(2 * HEAD_DIM, 2 * HEAD_DIM)], w_all.at[pl.ds(HEAD_DIM, 2 * HEAD_DIM)])]
    copies = start(sems, pairs)
    wait(copies[:3])
    block, step = q_ref.shape[0], HEAD_DIM
    for first in range(0, block, step):
        upto = first + step
        rows = slice(first, upto)
        at_q = first + lax.broadcasted_iota(jnp.int32, (step, 1), 0)
        at_k = lax.broadcasted_iota(jnp.int32, (1, upto), 1)
        for h in (0, 2, 3):
            weights, denom, peak = weigh(dot_t(q_all[rows, head(h)], k_all[:upto, head(h)]), at_k <= at_q)
            total = dot(weights, v_all[:upto, head(h)])
            if h == 0:
                row_ref[rows] = (total / denom).astype(BF16)
            else:
                sum_ref[h - 2, rows] = total
                low = lax.broadcasted_iota(jnp.int32, (step, HEAD_DIM), 1) < HEAD_DIM // 2
                stat_ref[h - 2, rows] = jnp.where(low, denom, peak)
    wait(copies[3:])


def own_part(queries, keys, values, out_weight):
    block = queries.shape[0]
    state = (VMEM, (2, block, HEAD_DIM), F32)
    weight_shape = (3 * HEAD_DIM, out_weight.shape[1])
    return call(
        own_kernel,
        [(VMEM, (block, HEAD_DIM)), state, state, (VMEM, (block, 2 * HEAD_DIM)), (VMEM, weight_shape)],
        [(HBM, x) for x in (queries, keys, values, out_weight)],
        [pltpu.VMEM(queries.shape, BF16)] * 3,
        6,
        room=OWN_ROOM,
    )


def part_kernel(flips, parts, slots, row_ref, sum_ref, stat_ref, q_ref, w_ref, mult_ref, *refs):
    tails, refs = refs[: len(slots)], refs[len(slots) :]
    outs, (far, sems) = refs[: len(flips)], refs[len(flips) :]
    pairs, at = [], 0
    for tail, many in zip(tails, slots):
        pairs.append((tail, far.at[pl.ds(at, many)]))
        at += many
    wait(start(sems, pairs))
    rows = q_ref.shape[0] // parts
    me = lax.axis_index("head")
    away_kv = [far[:, i].reshape(at * SUMMARY, HEAD_DIM) for i in range(4)]
    for flip, out_ref in zip(flips, outs):
        here = pl.ds(pl.multiple_of((me ^ flip) * rows, rows), rows)
        found = [row_ref[here, :]]
        for f in range(2):
            mult = mult_ref[f : f + 1, :]
            away = jnp.where(mult > 0, dot_t(q_ref[here, head(f)], away_kv[f]), NEG)
            own_denom, own_peak = stat_ref[f, here, :1], stat_ref[f, here, HEAD_DIM // 2 : HEAD_DIM // 2 + 1]
            peak = jnp.maximum(own_peak, jnp.max(away, axis=1, keepdims=True))
            shrink = jnp.exp2((own_peak - peak) * SCALE2)
            away = jnp.exp2((away - peak) * SCALE2) * mult
            denom = own_denom * shrink + jnp.sum(away, axis=1, keepdims=True)
            total = sum_ref[f, here, :] * shrink + dot(away.astype(BF16), away_kv[2 + f])
            found.append((total / denom).astype(BF16))
        out_ref[...] = dot(jnp.concatenate(found, axis=1), w_ref[...]).astype(BF16)


def add_kernel(a_ref, b_ref, out_ref, _):
    out_ref[...] = (a_ref[...].astype(F32) + b_ref[...].astype(F32)).astype(BF16)


def join_kernel(*refs):
    at = 0
    for ref in refs[:-2]:
        refs[-2][at : at + ref.shape[0]] = ref[...]
        at += ref.shape[0]


def near_kernel(own_ref, core_ref, moved_ref, *refs):
    ws, (out_ref, moved, sems) = refs[:-3], refs[-3:]
    wait(start(sems, [(moved_ref, moved)]))
    outer, heads, inner, depth = moved.shape
    me = lax.axis_index("head")
    total = own_ref[...].astype(F32) + core_ref[...].astype(F32)
    for i, w in enumerate(ws):
        total += dot(moved[:, me ^ i].reshape(outer * inner, depth), w[...])
    out_ref[...] = total


def last_kernel(near_ref, far_ref, out_ref, near, far, done, sems):
    pieces = sems.shape[0] // 3
    cut = done.shape[1] // pieces
    cols = [pl.ds(i * cut, cut) for i in range(pieces)]
    copies = start(sems, [(a.at[:, c], b.at[:, c]) for c in cols for a, b in ((near_ref, near), (far_ref, far))])
    sent = []
    for i, c in enumerate(cols):
        wait(copies[2 * i : 2 * i + 2])
        done[:, c] = (near[:, c] + far[:, c].astype(F32)).astype(BF16)
        sent += start(sems, [(done.at[:, c], out_ref.at[:, c])], 2 * pieces + i)
    wait(sent)


def swap(x, axis, flip, count):
    return lax.ppermute(x, axis, [(i, i ^ flip) for i in range(count)])


def gather_tails(mine, count):
    order, arrays = [0], [mine[None]]
    bits = [(count // 4**i, 4) for i in range(1, 8) if count % 4**i == 0 and count // 4**i >= 2] + [(1, 2)]
    if count & (count - 1) or bits[-2:][0][0] != 2:
        return [lax.all_gather(mine, "seq")], None
    for step, radix in bits:
        held = arrays[0]
        if len(arrays) > 1:
            shape = (sum(x.shape[0] for x in arrays), *mine.shape)
            (held,) = call(join_kernel, [(VMEM, shape)], [(VMEM, x) for x in arrays], cost=JOIN_COST)
        arrays = [held] + [swap(held, "seq", step * i, count) for i in range(1, radix)]
        order = [j ^ (step * i) for i in range(radix) for j in order]
    return arrays, order


def per_device(queries, keys, values, summary_lists, out_weight):
    count, parts = lax.axis_size("seq"), lax.axis_size("head")
    block = queries.shape[0]
    me = lax.axis_index("seq")
    per = block // (count * parts)
    columns = per * parts

    packed, tail, w_col = pack(queries, keys, values, out_weight, count, parts, per)
    tails, order = gather_tails(tail, count)

    moved = lax.all_to_all(
        packed.reshape(count, 3 * columns, HEAD_DIM), "seq", split_axis=0, concat_axis=0, tiled=True
    )
    moved = moved.reshape(count, 3, columns, HEAD_DIM)
    if columns % 16:
        moved = moved.transpose(1, 0, 2, 3).reshape(1, 3, block, HEAD_DIM)

    held = [queries, keys, values, out_weight, w_col]
    if len(tails) > 1:
        *held, tails[0] = lax.optimization_barrier((*held, tails[0]))
    w_col = held[4]
    w_far = swap(w_col, "head", 2, parts)
    w_core = swap(w_col, "head", 1, parts)
    w_both = swap(w_far, "head", 1, parts)

    slot_block = jnp.arange(count, dtype=jnp.int32) if order is None else me ^ jnp.array(order, jnp.int32)
    names = (summary_lists[0][:, :, None] == slot_block) & (slot_block < me)
    mult = jnp.repeat(jnp.sum(names.astype(F32), axis=1), SUMMARY, axis=1)

    shape = (block // parts, out_weight.shape[1])
    own = own_part(*held[:4])

    column_shape = (moved.shape[0], moved.shape[2], HEAD_DIM)
    (column_out,) = call(
        functools.partial(column_kernel, columns),
        [(HBM, column_shape)],
        [(HBM, moved)],
        [pltpu.VMEM((3, *column_shape), BF16), pltpu.VMEM(column_shape, BF16)],
        3,
        COLUMN_COST,
    )

    def partial_sums(flips):
        return call(
            functools.partial(part_kernel, flips, parts, [x.shape[0] for x in tails]),
            [(VMEM, shape)] * len(flips),
            [(VMEM, x) for x in (*own, mult)] + [(HBM, x) for x in tails],
            [pltpu.VMEM((count, 4, SUMMARY, HEAD_DIM), BF16)],
            len(tails),
        )

    both_sum, far_sum = partial_sums((3, 2))
    both_in = swap(both_sum, "head", 1, parts)
    (far_sum,) = call(add_kernel, [(VMEM, shape)], [(VMEM, far_sum), (VMEM, both_in)])
    far_in = swap(far_sum, "head", 2, parts)
    core_sum, own_sum = partial_sums((1, 0))
    core_in = swap(core_sum, "head", 1, parts)

    column_out = column_out.reshape(count * parts, per, HEAD_DIM)
    back = lax.all_to_all(column_out, ("seq", "head"), split_axis=0, concat_axis=0, tiled=True)
    back = back.reshape(count, parts, per, HEAD_DIM)
    if per % 16:
        back = back.transpose(1, 0, 2, 3).reshape(1, parts, count * per, HEAD_DIM)
    (near_sum,) = call(
        near_kernel,
        [(VMEM, shape, F32)],
        [(VMEM, own_sum), (VMEM, core_in), (HBM, back)] + [(VMEM, x) for x in (w_col, w_core, w_far, w_both)],
        [pltpu.VMEM(back.shape, BF16)],
        cost=LAST_COST,
    )
    (mixed,) = call(
        last_kernel,
        [(HBM, shape)],
        [(HBM, near_sum), (HBM, far_in)],
        [pltpu.VMEM(shape, F32), pltpu.VMEM(shape, BF16), pltpu.VMEM(shape, BF16)],
        3 * 4,
    )
    return mixed


def solution(mesh):
    return jax.shard_map(
        per_device,
        mesh=mesh,
        in_specs=(
            P("seq", "head"),
            P("seq", "head"),
            P("seq", "head"),
            P("seq", "head", None),
            P("head", None),
        ),
        out_specs=P(("seq", "head"), None),
        check_vma=False,
    )
```

```python
import functools
import math

import jax
import jax.numpy as jnp
import numpy as np
from jax import lax
from jax.experimental import pallas as pl
from jax.experimental.pallas import tpu as pltpu
from jax.sharding import PartitionSpec as P

HEAD_DIM = 128
SUMMARY = 32
NEG = -1e30
JOIN_COST = 10**9
COLUMN_COST = 10**9*3
OWN_ROOM = 48
BF16 = jnp.bfloat16
F32 = jnp.float32
HBM = pl.BlockSpec(memory_space=pltpu.HBM)
VMEM = pl.BlockSpec(memory_space=pltpu.VMEM)
SMEM = pl.BlockSpec(memory_space=pltpu.SMEM)
SCALE2 = HEAD_DIM ** (-0.5) * math.log2(math.e)


def call(kernel, out, operands, scratch=(), copies=1, cost=1, room=24):
    return pl.pallas_call(
        kernel,
        out_shape=[jax.ShapeDtypeStruct(x[1], x[2] if len(x) > 2 else BF16) for x in out],
        in_specs=[memory for memory, _ in operands],
        out_specs=[x[0] for x in out],
        scratch_shapes=[*scratch, pltpu.SemaphoreType.DMA((copies,))],
        compiler_params=pltpu.CompilerParams(vmem_limit_bytes=room * 2**20),
        cost_estimate=pl.CostEstimate(flops=cost, bytes_accessed=1, transcendentals=0),
    )(*(x for _, x in operands))


def start(sems, pairs, first=0):
    copies = [pltpu.make_async_copy(src, dst, sems.at[first + i]) for i, (src, dst) in enumerate(pairs)]
    for copy in copies:
        copy.start()
    return copies


def wait(copies):
    for copy in copies:
        copy.wait()


def dot_t(a, b):
    return lax.dot_general(a, b, (((1,), (1,)), ((), ())), preferred_element_type=F32)


def dot(a, b):
    return jnp.dot(a, b, preferred_element_type=F32)


def weigh(scores, valid):
    scores = jnp.where(valid, scores, NEG)
    peak = jnp.max(scores, axis=1, keepdims=True)
    weights = jnp.exp2((scores - peak) * SCALE2)
    return weights.astype(BF16), jnp.sum(weights, axis=1, keepdims=True), peak


def head(h):
    return slice(h * HEAD_DIM, (h + 1) * HEAD_DIM)


def pack_kernel(q_ref, k_ref, v_ref, w_ref, tail_ref, packed_ref, w_col_ref, tail, cols, w_col, sems):
    parts, count, per, _ = q_ref.shape
    near = pl.ds(count - SUMMARY // per, SUMMARY // per)
    come = []
    for i, ref in enumerate((k_ref, v_ref)):
        for f in range(2):
            come.append((ref.at[parts - 1, near, :, pl.ds((2 + f) * HEAD_DIM, HEAD_DIM)], tail.at[2 * i + f]))
    for i, ref in enumerate((q_ref, k_ref, v_ref)):
        come.append((ref.at[:, :, :, pl.ds(HEAD_DIM, HEAD_DIM)], cols.at[i]))
    come = start(sems, come + [(w_ref.at[pl.ds(HEAD_DIM, HEAD_DIM)], w_col)])
    first = len(come)
    wait(come[:4])
    gone = start(sems, [(tail, tail_ref)], first)
    for i, copy in enumerate(come[4:7]):
        wait([copy])
        pairs = [(cols.at[i, j], packed_ref.at[:, i, j]) for j in range(parts)]
        gone += start(sems, pairs, first + 1 + i * parts)
    wait(come[7:])
    gone += start(sems, [(w_col, w_col_ref)], first + 1 + 3 * parts)
    wait(gone)


def tail_kernel(k_ref, v_ref, tail, sems):
    block = k_ref.shape[0]
    pairs = []
    for i, ref in enumerate((k_ref, v_ref)):
        for f in range(2):
            pairs.append((ref.at[pl.ds(block - SUMMARY, SUMMARY), pl.ds((2 + f) * HEAD_DIM, HEAD_DIM)], tail.at[2 * i + f]))
    wait(start(sems, pairs))


def pack(queries, keys, values, out_weight, count, parts, per):
    width = queries.shape[1]
    tail_shape = (4, SUMMARY, HEAD_DIM)
    if per % 16:
        (tail,) = call(tail_kernel, [(VMEM, tail_shape)], [(HBM, keys), (HBM, values)], (), 4, room=63)
        cut = [x[:, HEAD_DIM : 2 * HEAD_DIM].reshape(parts, count, per, HEAD_DIM) for x in (queries, keys, values)]
        packed = jnp.stack(cut).transpose(2, 0, 1, 3, 4)
        return packed, tail, out_weight[HEAD_DIM : 2 * HEAD_DIM]
    tail_cut, w_shape = (4, SUMMARY // per, per, HEAD_DIM), (HEAD_DIM, out_weight.shape[1])
    tail, packed, w_col = call(
        pack_kernel,
        [(HBM, tail_cut), (HBM, (count, 3, parts, per, HEAD_DIM)), (HBM, w_shape)],
        [(HBM, x.reshape(parts, count, per, width)) for x in (queries, keys, values)] + [(HBM, out_weight)],
        [pltpu.VMEM(tail_cut, BF16), pltpu.VMEM((3, parts, count, per, HEAD_DIM), BF16), pltpu.VMEM(w_shape, BF16)],
        10 + 3 * parts,
        room=63,
    )
    return packed, tail.reshape(tail_shape), w_col


def column_kernel(columns, moved_ref, out_ref, held, done, sems):
    outer, _, inner, depth = moved_ref.shape
    rows = outer * inner
    copies = start(sems, [(moved_ref.at[:, i], held.at[i]) for i in range(3)])
    wait(copies[:2])
    q, k, v = (held.at[i] for i in range(3))
    step = HEAD_DIM
    results = []
    for first in range(0, rows, step):
        upto = first + step
        at_q = first + lax.broadcasted_iota(jnp.int32, (step, 1), 0)
        at_k = lax.broadcasted_iota(jnp.int32, (1, upto), 1)
        valid = (lax.rem(at_q, columns) == lax.rem(at_k, columns)) & (at_k <= at_q)
        q_rows = q[...].reshape(rows, depth)[first:upto]
        results.append((upto, *weigh(dot_t(q_rows, k[...].reshape(rows, depth)[:upto]), valid)))
    wait(copies[2:])
    out = [dot(weights, v[...].reshape(rows, depth)[:upto]) / denom for upto, weights, denom, _ in results]
    done[...] = jnp.concatenate(out, axis=0).astype(BF16).reshape(outer, inner, depth)
    wait(start(sems, [(done, out_ref)]))


def own_kernel(relative, q_ref, k_ref, v_ref, w_ref, lists_ref, slots_ref, row_ref, sum_ref, stat_ref, q_fixed, w_all, mult_ref, q_all, k_all, v_all, sems):
    pairs = [(q_ref, q_all), (k_ref, k_all), (v_ref, v_all)]
    pairs += [(q_ref.at[:, pl.ds(2 * HEAD_DIM, 2 * HEAD_DIM)], q_fixed)]
    pairs += [(w_ref.at[pl.ds(0, HEAD_DIM)], w_all.at[pl.ds(0, HEAD_DIM)])]
    pairs += [(w_ref.at[pl.ds(2 * HEAD_DIM, 2 * HEAD_DIM)], w_all.at[pl.ds(HEAD_DIM, 2 * HEAD_DIM)])]
    copies = start(sems, pairs)
    me = lax.axis_index("seq")
    tile = slots_ref[...] ^ me if relative else slots_ref[...]
    for f in range(2):
        times = sum((tile == lists_ref[f, i]).astype(F32) for i in range(lists_ref.shape[1]))
        mult_ref[f : f + 1, :] = jnp.where(tile < me, times, 0.0)
    wait(copies[:3])
    block, step = q_ref.shape[0], HEAD_DIM
    for first in range(0, block, step):
        upto = first + step
        rows = slice(first, upto)
        at_q = first + lax.broadcasted_iota(jnp.int32, (step, 1), 0)
        at_k = lax.broadcasted_iota(jnp.int32, (1, upto), 1)
        for h in (0, 2, 3):
            weights, denom, peak = weigh(dot_t(q_all[rows, head(h)], k_all[:upto, head(h)]), at_k <= at_q)
            total = dot(weights, v_all[:upto, head(h)])
            if h == 0:
                row_ref[rows] = (total / denom).astype(BF16)
            else:
                sum_ref[h - 2, rows] = total
                low = lax.broadcasted_iota(jnp.int32, (step, HEAD_DIM), 1) < HEAD_DIM // 2
                stat_ref[h - 2, rows] = jnp.where(low, denom, peak)
    wait(copies[3:])


def own_part(queries, keys, values, out_weight, lists, slots, relative):
    block = queries.shape[0]
    state = (VMEM, (2, block, HEAD_DIM), F32)
    weight_shape = (3 * HEAD_DIM, out_weight.shape[1])
    return call(
        functools.partial(own_kernel, relative),
        [(VMEM, (block, HEAD_DIM)), state, state, (VMEM, (block, 2 * HEAD_DIM)), (VMEM, weight_shape), (VMEM, (2, slots.shape[1]), F32)],
        [(HBM, x) for x in (queries, keys, values, out_weight)] + [(SMEM, lists), (VMEM, jnp.array(slots))],
        [pltpu.VMEM(queries.shape, BF16)] * 3,
        6,
        room=OWN_ROOM,
    )


def part_kernel(flips, parts, slots, row_ref, sum_ref, stat_ref, q_ref, w_ref, mult_ref, *refs):
    tails, refs = refs[: len(slots)], refs[len(slots) :]
    outs, (far, sems) = refs[: len(flips)], refs[len(flips) :]
    pairs, at = [], 0
    for tail, many in zip(tails, slots):
        pairs.append((tail, far.at[pl.ds(at, many)]))
        at += many
    wait(start(sems, pairs))
    rows = q_ref.shape[0] // parts
    me = lax.axis_index("head")
    away_kv = [far[:, i].reshape(at * SUMMARY, HEAD_DIM) for i in range(4)]
    for flip, out_ref in zip(flips, outs):
        here = pl.ds(pl.multiple_of((me ^ flip) * rows, rows), rows)
        found = [row_ref[here, :]]
        for f in range(2):
            mult = mult_ref[f : f + 1, :]
            away = jnp.where(mult > 0, dot_t(q_ref[here, head(f)], away_kv[f]), NEG)
            own_denom, own_peak = stat_ref[f, here, :1], stat_ref[f, here, HEAD_DIM // 2 : HEAD_DIM // 2 + 1]
            peak = jnp.maximum(own_peak, jnp.max(away, axis=1, keepdims=True))
            shrink = jnp.exp2((own_peak - peak) * SCALE2)
            away = jnp.exp2((away - peak) * SCALE2) * mult
            denom = own_denom * shrink + jnp.sum(away, axis=1, keepdims=True)
            total = sum_ref[f, here, :] * shrink + dot(away.astype(BF16), away_kv[2 + f])
            found.append((total / denom).astype(BF16))
        out_ref[...] = dot(jnp.concatenate(found, axis=1), w_ref[...]).astype(BF16)


def add_kernel(a_ref, b_ref, out_ref, done, sems):
    pieces = sems.shape[0]
    cut = done.shape[0] // pieces
    sent = []
    for i in range(pieces):
        rows = pl.ds(i * cut, cut)
        done[rows] = (a_ref[rows, :].astype(F32) + b_ref[rows, :].astype(F32)).astype(BF16)
        sent += start(sems, [(done.at[rows], out_ref.at[rows])], i)
    wait(sent)


def join_kernel(*refs):
    at = 0
    for ref in refs[:-2]:
        refs[-2][at : at + ref.shape[0]] = ref[...]
        at += ref.shape[0]


def last_kernel(own_ref, core_ref, far_ref, moved_ref, *refs):
    ws, (out_ref, moved, far, done, sems) = refs[:-5], refs[-5:]
    pieces = (sems.shape[0] - 1) // 2
    cut = done.shape[1] // pieces
    cols = [pl.ds(i * cut, cut) for i in range(pieces)]
    first, *copies = start(sems, [(moved_ref, moved)] + [(far_ref.at[:, c], far.at[:, c]) for c in cols])
    outer, heads, inner, depth = moved.shape
    me = lax.axis_index("head")
    wait([first])
    found = jnp.concatenate([moved[:, me ^ i].reshape(outer * inner, depth) for i in range(heads)], axis=1)
    sent = []
    for i, c in enumerate(cols):
        total = dot(found, jnp.concatenate([w[:, c] for w in ws], axis=0))
        total += own_ref[:, c].astype(F32) + core_ref[:, c].astype(F32)
        wait(copies[i : i + 1])
        done[:, c] = (total + far[:, c].astype(F32)).astype(BF16)
        sent += start(sems, [(done.at[:, c], out_ref.at[:, c])], 1 + pieces + i)
    wait(sent)


def swap(x, axis, flip, count):
    return lax.ppermute(x, axis, [(i, i ^ flip) for i in range(count)])


def gather_tails(mine, count):
    bits = [(count // 4**i, 4) for i in range(1, 8) if count % 4**i == 0 and count // 4**i >= 2] + [(1, 2)]
    if count & (count - 1) or bits[-2:][0][0] != 2:
        return [lax.all_gather(mine, "seq")], None
    order, arrays = [0], [mine[None]]
    for step, radix in bits:
        if len(arrays) > 1:
            shape = (sum(x.shape[0] for x in arrays[1:]), *mine.shape)
            (came,) = call(join_kernel, [(VMEM, shape)], [(VMEM, x) for x in arrays[1:]], cost=JOIN_COST)
            arrays = list(lax.optimization_barrier((arrays[0], came)))
        if step == 1 or len(arrays) == 1:
            arrays += [swap(x, "seq", step * i, count) for i in range(1, radix) for x in arrays]
        else:
            held = jnp.concatenate(arrays, axis=0)
            arrays = [held] + [swap(held, "seq", step * i, count) for i in range(1, radix)]
        order = [j ^ (step * i) for i in range(radix) for j in order]
    return arrays, order


def per_device(queries, keys, values, summary_lists, out_weight):
    count, parts = lax.axis_size("seq"), lax.axis_size("head")
    block = queries.shape[0]
    me = lax.axis_index("seq")
    per = block // (count * parts)
    columns = per * parts

    packed, tail, w_col = pack(queries, keys, values, out_weight, count, parts, per)
    tails, order = gather_tails(tail, count)

    moved = lax.all_to_all(
        packed.reshape(count, 3 * columns, HEAD_DIM), "seq", split_axis=0, concat_axis=0, tiled=True
    )
    moved = moved.reshape(count, 3, columns, HEAD_DIM)
    if columns % 16:
        moved = moved.transpose(1, 0, 2, 3).reshape(1, 3, block, HEAD_DIM)

    held = [queries, keys, values, out_weight, w_col]
    if len(tails) > 1:
        *held, tails[0] = lax.optimization_barrier((*held, tails[0]))
    w_col = held[4]
    w_far = swap(w_col, "head", 2, parts)
    w_core = swap(w_col, "head", 1, parts)
    w_both = swap(w_far, "head", 1, parts)

    slots = np.repeat(np.arange(count) if order is None else np.array(order), SUMMARY)[None].astype(np.int32)
    shape = (block // parts, out_weight.shape[1])
    *own, mult = own_part(*held[:4], summary_lists[0], slots, order is not None)

    def partial_sums(flips):
        return call(
            functools.partial(part_kernel, flips, parts, [x.shape[0] for x in tails]),
            [(VMEM, shape)] * len(flips),
            [(VMEM, x) for x in (*own, mult)] + [(HBM, x) for x in tails],
            [pltpu.VMEM((count, 4, SUMMARY, HEAD_DIM), BF16)],
            len(tails),
        )

    both_sum, far_sum = partial_sums((3, 2))
    both_in = swap(both_sum, "head", 1, parts)
    (far_sum,) = call(add_kernel, [(HBM, shape)], [(VMEM, far_sum), (VMEM, both_in)], [pltpu.VMEM(shape, BF16)], 4)
    moved, _ = lax.optimization_barrier((moved, far_sum))
    column_shape = (moved.shape[0], moved.shape[2], HEAD_DIM)
    (column_out,) = call(
        functools.partial(column_kernel, columns),
        [(HBM, column_shape)],
        [(HBM, moved)],
        [pltpu.VMEM((3, *column_shape), BF16), pltpu.VMEM(column_shape, BF16)],
        3,
        COLUMN_COST,
    )

    far_in = swap(far_sum, "head", 2, parts)
    core_sum, own_sum = partial_sums((1, 0))
    core_in = swap(core_sum, "head", 1, parts)

    column_out = column_out.reshape(count * parts, per, HEAD_DIM)
    back = lax.all_to_all(column_out, ("seq", "head"), split_axis=0, concat_axis=0, tiled=True)
    back = back.reshape(count, parts, per, HEAD_DIM)
    if per % 16:
        back = back.transpose(1, 0, 2, 3).reshape(1, parts, count * per, HEAD_DIM)
    (mixed,) = call(
        last_kernel,
        [(HBM, shape)],
        [(VMEM, own_sum), (VMEM, core_in), (HBM, far_in), (HBM, back)] + [(VMEM, x) for x in (w_col, w_core, w_far, w_both)],
        [pltpu.VMEM(back.shape, BF16), pltpu.VMEM(shape, BF16), pltpu.VMEM(shape, BF16)],
        1 + 2 * 1,
    )
    return mixed


def solution(mesh):
    return jax.shard_map(
        per_device,
        mesh=mesh,
        in_specs=(
            P("seq", "head"),
            P("seq", "head"),
            P("seq", "head"),
            P("seq", "head", None),
            P("head", None),
        ),
        out_specs=P(("seq", "head"), None),
        check_vma=False,
    )
```

```python
import functools
import math

import jax
import jax.numpy as jnp
import numpy as np
from jax import lax
from jax.experimental import pallas as pl
from jax.experimental.pallas import tpu as pltpu
from jax.sharding import PartitionSpec as P

HEAD_DIM = 128
SUMMARY = 32
NEG = -1e30
JOIN_COST = 10**9
COLUMN_COST = 10**9*3
OWN_ROOM = 48
SETTLE_COST = 25*10**8
BF16 = jnp.bfloat16
F32 = jnp.float32
HBM = pl.BlockSpec(memory_space=pltpu.HBM)
VMEM = pl.BlockSpec(memory_space=pltpu.VMEM)
SMEM = pl.BlockSpec(memory_space=pltpu.SMEM)
SCALE2 = HEAD_DIM ** (-0.5) * math.log2(math.e)


def call(kernel, out, operands, scratch=(), copies=1, cost=1, room=24):
    return pl.pallas_call(
        kernel,
        out_shape=[jax.ShapeDtypeStruct(x[1], x[2] if len(x) > 2 else BF16) for x in out],
        in_specs=[memory for memory, _ in operands],
        out_specs=[x[0] for x in out],
        scratch_shapes=[*scratch, pltpu.SemaphoreType.DMA((copies,))],
        compiler_params=pltpu.CompilerParams(vmem_limit_bytes=room * 2**20),
        cost_estimate=pl.CostEstimate(flops=cost, bytes_accessed=1, transcendentals=0),
    )(*(x for _, x in operands))


def start(sems, pairs, first=0):
    copies = [pltpu.make_async_copy(src, dst, sems.at[first + i]) for i, (src, dst) in enumerate(pairs)]
    for copy in copies:
        copy.start()
    return copies


def wait(copies):
    for copy in copies:
        copy.wait()


def dot_t(a, b):
    return lax.dot_general(a, b, (((1,), (1,)), ((), ())), preferred_element_type=F32)


def dot(a, b):
    return jnp.dot(a, b, preferred_element_type=F32)


def weigh(scores, valid):
    scores = jnp.where(valid, scores, NEG)
    peak = jnp.max(scores, axis=1, keepdims=True)
    weights = jnp.exp2((scores - peak) * SCALE2)
    return weights.astype(BF16), jnp.sum(weights, axis=1, keepdims=True), peak


def head(h):
    return slice(h * HEAD_DIM, (h + 1) * HEAD_DIM)


def pack_kernel(q_ref, k_ref, v_ref, w_ref, tail_ref, packed_ref, w_col_ref, tail, cols, w_col, sems):
    parts, count, per, _ = q_ref.shape
    near = pl.ds(count - SUMMARY // per, SUMMARY // per)
    come = []
    for i, ref in enumerate((k_ref, v_ref)):
        for f in range(2):
            come.append((ref.at[parts - 1, near, :, pl.ds((2 + f) * HEAD_DIM, HEAD_DIM)], tail.at[2 * i + f]))
    for i, ref in enumerate((q_ref, k_ref, v_ref)):
        come.append((ref.at[:, :, :, pl.ds(HEAD_DIM, HEAD_DIM)], cols.at[i]))
    quarter = HEAD_DIM // 4
    for i in range(4):
        come.append((w_ref.at[pl.ds(HEAD_DIM + i * quarter, quarter)], w_col.at[pl.ds(i * quarter, quarter)]))
    come = start(sems, come)
    first = len(come)
    wait(come[:4])
    gone = start(sems, [(tail, tail_ref)], first)
    for i, copy in enumerate(come[4:7]):
        wait([copy])
        pairs = [(cols.at[i, j], packed_ref.at[:, i, j]) for j in range(parts)]
        gone += start(sems, pairs, first + 1 + i * parts)
    for i, copy in enumerate(come[7:]):
        wait([copy])
        rows = pl.ds(i * quarter, quarter)
        gone += start(sems, [(w_col.at[rows], w_col_ref.at[rows])], first + 1 + 3 * parts + i)
    wait(gone)


def tail_kernel(k_ref, v_ref, tail, sems):
    block = k_ref.shape[0]
    pairs = []
    for i, ref in enumerate((k_ref, v_ref)):
        for f in range(2):
            pairs.append((ref.at[pl.ds(block - SUMMARY, SUMMARY), pl.ds((2 + f) * HEAD_DIM, HEAD_DIM)], tail.at[2 * i + f]))
    wait(start(sems, pairs))


def pack(queries, keys, values, out_weight, count, parts, per):
    width = queries.shape[1]
    tail_shape = (4, SUMMARY, HEAD_DIM)
    if per % 16:
        (tail,) = call(tail_kernel, [(VMEM, tail_shape)], [(HBM, keys), (HBM, values)], (), 4, room=63)
        cut = [x[:, HEAD_DIM : 2 * HEAD_DIM].reshape(parts, count, per, HEAD_DIM) for x in (queries, keys, values)]
        packed = jnp.stack(cut).transpose(2, 0, 1, 3, 4)
        return packed, tail, out_weight[HEAD_DIM : 2 * HEAD_DIM]
    tail_cut, w_shape = (4, SUMMARY // per, per, HEAD_DIM), (HEAD_DIM, out_weight.shape[1])
    tail, packed, w_col = call(
        pack_kernel,
        [(HBM, tail_cut), (HBM, (count, 3, parts, per, HEAD_DIM)), (HBM, w_shape)],
        [(HBM, x.reshape(parts, count, per, width)) for x in (queries, keys, values)] + [(HBM, out_weight)],
        [pltpu.VMEM(tail_cut, BF16), pltpu.VMEM((3, parts, count, per, HEAD_DIM), BF16), pltpu.VMEM(w_shape, BF16)],
        16 + 3 * parts,
        room=63,
    )
    return packed, tail.reshape(tail_shape), w_col


def column_kernel(columns, moved_ref, out_ref, held, done, sems):
    outer, _, inner, depth = moved_ref.shape
    rows = outer * inner
    copies = start(sems, [(moved_ref.at[:, i], held.at[i]) for i in range(3)])
    wait(copies[:2])
    q, k, v = (held.at[i] for i in range(3))
    step = HEAD_DIM
    results = []
    for first in range(0, rows, step):
        upto = first + step
        at_q = first + lax.broadcasted_iota(jnp.int32, (step, 1), 0)
        at_k = lax.broadcasted_iota(jnp.int32, (1, upto), 1)
        valid = (lax.rem(at_q, columns) == lax.rem(at_k, columns)) & (at_k <= at_q)
        q_rows = q[...].reshape(rows, depth)[first:upto]
        results.append((upto, *weigh(dot_t(q_rows, k[...].reshape(rows, depth)[:upto]), valid)))
    wait(copies[2:])
    out = [dot(weights, v[...].reshape(rows, depth)[:upto]) / denom for upto, weights, denom, _ in results]
    done[...] = jnp.concatenate(out, axis=0).astype(BF16).reshape(outer, inner, depth)
    wait(start(sems, [(done, out_ref)]))


def own_kernel(relative, q_ref, k_ref, v_ref, w_ref, lists_ref, slots_ref, row_ref, sum_ref, stat_ref, q_fixed, w_all, mult_ref, q_all, k_all, v_all, sems):
    pairs = [(q_ref, q_all), (k_ref, k_all), (v_ref, v_all)]
    pairs += [(q_ref.at[:, pl.ds(2 * HEAD_DIM, 2 * HEAD_DIM)], q_fixed)]
    pairs += [(w_ref.at[pl.ds(0, HEAD_DIM)], w_all.at[pl.ds(0, HEAD_DIM)])]
    pairs += [(w_ref.at[pl.ds(2 * HEAD_DIM, 2 * HEAD_DIM)], w_all.at[pl.ds(HEAD_DIM, 2 * HEAD_DIM)])]
    copies = start(sems, pairs)
    me = lax.axis_index("seq")
    tile = slots_ref[...] ^ me if relative else slots_ref[...]
    for f in range(2):
        times = sum((tile == lists_ref[f, i]).astype(F32) for i in range(lists_ref.shape[1]))
        mult_ref[f : f + 1, :] = jnp.where(tile < me, times, 0.0)
    wait(copies[:3])
    block, step = q_ref.shape[0], HEAD_DIM
    for first in range(0, block, step):
        upto = first + step
        rows = slice(first, upto)
        at_q = first + lax.broadcasted_iota(jnp.int32, (step, 1), 0)
        at_k = lax.broadcasted_iota(jnp.int32, (1, upto), 1)
        for h in (0, 2, 3):
            weights, denom, peak = weigh(dot_t(q_all[rows, head(h)], k_all[:upto, head(h)]), at_k <= at_q)
            total = dot(weights, v_all[:upto, head(h)])
            if h == 0:
                row_ref[rows] = (total / denom).astype(BF16)
            else:
                sum_ref[h - 2, rows] = total
                low = lax.broadcasted_iota(jnp.int32, (step, HEAD_DIM), 1) < HEAD_DIM // 2
                stat_ref[h - 2, rows] = jnp.where(low, denom, peak)
    wait(copies[3:])


def own_part(queries, keys, values, out_weight, lists, slots, relative):
    block = queries.shape[0]
    state = (VMEM, (2, block, HEAD_DIM), F32)
    weight_shape = (3 * HEAD_DIM, out_weight.shape[1])
    return call(
        functools.partial(own_kernel, relative),
        [(VMEM, (block, HEAD_DIM)), state, state, (VMEM, (block, 2 * HEAD_DIM)), (VMEM, weight_shape), (VMEM, (2, slots.shape[1]), F32)],
        [(HBM, x) for x in (queries, keys, values, out_weight)] + [(SMEM, lists), (VMEM, jnp.array(slots))],
        [pltpu.VMEM(queries.shape, BF16)] * 3,
        6,
        room=OWN_ROOM,
    )


def part_kernel(flips, parts, row_ref, sum_ref, stat_ref, q_ref, w_ref, mult_ref, *refs):
    tails, outs = refs[: -len(flips) - 1], refs[-len(flips) - 1 : -1]
    rows = q_ref.shape[0] // parts
    me = lax.axis_index("head")
    away_kv = [
        jnp.concatenate([x[:, i].reshape(x.shape[0] * SUMMARY, HEAD_DIM) for x in tails], axis=0) for i in range(4)
    ]
    here = [pl.ds(pl.multiple_of((me ^ flip) * rows, rows), rows) for flip in flips]
    items = [(at, f) for at in here for f in range(2)]
    mult = [mult_ref[f : f + 1, :] for f in range(2)]
    ones = jnp.ones_like(away_kv[0])
    values = [jnp.concatenate([away_kv[2 + f], ones], axis=1) for f in range(2)]
    away = [jnp.where(mult[f] > 0, dot_t(q_ref[at, head(f)], away_kv[f]), NEG) for at, f in items]
    own_peak = [stat_ref[f, at, HEAD_DIM // 2 : HEAD_DIM // 2 + 1] for at, f in items]
    peak = [jnp.maximum(x, jnp.max(y, axis=1, keepdims=True)) for x, y in zip(own_peak, away)]
    away = [(jnp.exp2((x - y) * SCALE2) * mult[f]).astype(BF16) for x, y, (_, f) in zip(away, peak, items)]
    total = [dot(x, values[f]) for x, (_, f) in zip(away, items)]
    shrink = [jnp.exp2((x - y) * SCALE2) for x, y in zip(own_peak, peak)]
    denom = [stat_ref[f, at, :1] * z + x[:, HEAD_DIM:] for (at, f), x, z in zip(items, total, shrink)]
    total = [sum_ref[f, at, :] * z + x[:, :HEAD_DIM] for (at, f), x, z in zip(items, total, shrink)]
    found = [(x / y).astype(BF16) for x, y in zip(total, denom)]
    for i, (at, out_ref) in enumerate(zip(here, outs)):
        out_ref[...] = dot(jnp.concatenate([row_ref[at, :], *found[2 * i : 2 * i + 2]], axis=1), w_ref[...]).astype(BF16)


def add_kernel(a_ref, b_ref, out_ref, done, sems):
    pieces = sems.shape[0]
    cut = done.shape[0] // pieces
    sent = []
    for i in range(pieces):
        rows = pl.ds(i * cut, cut)
        done[rows] = (a_ref[rows, :].astype(F32) + b_ref[rows, :].astype(F32)).astype(BF16)
        sent += start(sems, [(done.at[rows], out_ref.at[rows])], i)
    wait(sent)


def join_kernel(*refs):
    at = 0
    for ref in refs[:-2]:
        refs[-2][at : at + ref.shape[0]] = ref[...]
        at += ref.shape[0]


def last_kernel(own_ref, core_ref, far_ref, moved_ref, *refs):
    ws, (out_ref, moved, far, done, sems) = refs[:-6], refs[-5:]
    pieces = (sems.shape[0] - 1) // 2
    cut = done.shape[1] // pieces
    cols = [pl.ds(i * cut, cut) for i in range(pieces)]
    first, *copies = start(sems, [(moved_ref, moved)] + [(far_ref.at[:, c], far.at[:, c]) for c in cols])
    outer, heads, inner, depth = moved.shape
    me = lax.axis_index("head")
    wait([first])
    found = jnp.concatenate([moved[:, me ^ i].reshape(outer * inner, depth) for i in range(heads)], axis=1)
    sent = []
    for i, c in enumerate(cols):
        total = dot(found, jnp.concatenate([w[:, c] for w in ws], axis=0))
        total += own_ref[:, c].astype(F32) + core_ref[:, c].astype(F32)
        wait(copies[i : i + 1])
        done[:, c] = (total + far[:, c].astype(F32)).astype(BF16)
        sent += start(sems, [(done.at[:, c], out_ref.at[:, c])], 1 + pieces + i)
    wait(sent)


def settle_kernel(w_ref, out_ref, sems):
    wait(start(sems, [(w_ref.at[pl.ds(0, 16), pl.ds(0, HEAD_DIM)], out_ref)]))


def swap(x, axis, flip, count):
    return lax.ppermute(x, axis, [(i, i ^ flip) for i in range(count)])


def gather_tails(mine, count):
    bits = [(count // 4**i, 4) for i in range(1, 8) if count % 4**i == 0 and count // 4**i >= 2] + [(1, 2)]
    if count & (count - 1) or bits[-2:][0][0] != 2:
        return [lax.all_gather(mine, "seq")], None
    order, arrays = [0], [mine[None]]
    for step, radix in bits:
        if len(arrays) > 1:
            shape = (sum(x.shape[0] for x in arrays[1:]), *mine.shape)
            (came,) = call(join_kernel, [(VMEM, shape)], [(VMEM, x) for x in arrays[1:]], cost=JOIN_COST)
            arrays = list(lax.optimization_barrier((arrays[0], came)))
        if step == 1 or len(arrays) == 1:
            arrays += [swap(x, "seq", step * i, count) for i in range(1, radix) for x in arrays]
        else:
            held = jnp.concatenate(arrays, axis=0)
            arrays = [held] + [swap(held, "seq", step * i, count) for i in range(1, radix)]
        order = [j ^ (step * i) for i in range(radix) for j in order]
    return arrays, order


def per_device(queries, keys, values, summary_lists, out_weight):
    count, parts = lax.axis_size("seq"), lax.axis_size("head")
    block = queries.shape[0]
    me = lax.axis_index("seq")
    per = block // (count * parts)
    columns = per * parts

    packed, tail, w_col = pack(queries, keys, values, out_weight, count, parts, per)
    tails, order = gather_tails(tail, count)

    moved = lax.all_to_all(
        packed.reshape(count, 3 * columns, HEAD_DIM), "seq", split_axis=0, concat_axis=0, tiled=True
    )
    moved = moved.reshape(count, 3, columns, HEAD_DIM)
    if columns % 16:
        moved = moved.transpose(1, 0, 2, 3).reshape(1, 3, block, HEAD_DIM)

    held = [queries, keys, values, out_weight]
    if len(tails) > 1:
        *held, tails[0] = lax.optimization_barrier((*held, tails[0]))
    w_far = swap(w_col, "head", 2, parts)
    w_core = swap(w_col, "head", 1, parts)
    w_both = swap(w_far, "head", 1, parts)

    slots = np.repeat(np.arange(count) if order is None else np.array(order), SUMMARY)[None].astype(np.int32)
    shape = (block // parts, out_weight.shape[1])
    *own, mult = own_part(*held[:4], summary_lists[0], slots, order is not None)

    def partial_sums(flips):
        return call(
            functools.partial(part_kernel, flips, parts),
            [(VMEM, shape)] * len(flips),
            [(VMEM, x) for x in (*own, mult, *tails)],
        )

    both_sum, far_sum = partial_sums((3, 2))
    both_in = swap(both_sum, "head", 1, parts)
    (far_sum,) = call(add_kernel, [(HBM, shape)], [(VMEM, far_sum), (VMEM, both_in)], [pltpu.VMEM(shape, BF16)], 4)
    moved, _ = lax.optimization_barrier((moved, far_sum))
    column_shape = (moved.shape[0], moved.shape[2], HEAD_DIM)
    (column_out,) = call(
        functools.partial(column_kernel, columns),
        [(HBM, column_shape)],
        [(HBM, moved)],
        [pltpu.VMEM((3, *column_shape), BF16), pltpu.VMEM(column_shape, BF16)],
        3,
        COLUMN_COST,
    )

    far_in = swap(far_sum, "head", 2, parts)
    core_sum, own_sum = partial_sums((1, 0))
    core_in = swap(core_sum, "head", 1, parts)

    column_out = column_out.reshape(count * parts, per, HEAD_DIM)
    back = lax.all_to_all(column_out, ("seq", "head"), split_axis=0, concat_axis=0, tiled=True)
    back = back.reshape(count, parts, per, HEAD_DIM)
    if per % 16:
        back = back.transpose(1, 0, 2, 3).reshape(1, parts, count * per, HEAD_DIM)
    (settled,) = call(settle_kernel, [(VMEM, (16, HEAD_DIM))], [(HBM, w_both)], cost=SETTLE_COST)
    (mixed,) = call(
        last_kernel,
        [(HBM, shape)],
        [(VMEM, own_sum), (VMEM, core_in), (HBM, far_in), (HBM, back)] + [(VMEM, x) for x in (w_col, w_core, w_far, w_both, settled)],
        [pltpu.VMEM(back.shape, BF16), pltpu.VMEM(shape, BF16), pltpu.VMEM(shape, BF16)],
        1 + 2 * 1,
    )
    return mixed


def solution(mesh):
    return jax.shard_map(
        per_device,
        mesh=mesh,
        in_specs=(
            P("seq", "head"),
            P("seq", "head"),
            P("seq", "head"),
            P("seq", "head", None),
            P("head", None),
        ),
        out_specs=P(("seq", "head"), None),
        check_vma=False,
    )
```

```python
import functools
import math

import jax
import jax.numpy as jnp
import numpy as np
from jax import lax
from jax.experimental import pallas as pl
from jax.experimental.pallas import tpu as pltpu
from jax.sharding import PartitionSpec as P

HEAD_DIM = 128
SUMMARY = 32
NEG = -1e30
JOIN_COST = 10**9
COLUMN_COST = 10**9*3
OWN_ROOM = 48
SETTLE_COST = 25*10**8
BF16 = jnp.bfloat16
F32 = jnp.float32
HBM = pl.BlockSpec(memory_space=pltpu.HBM)
VMEM = pl.BlockSpec(memory_space=pltpu.VMEM)
SMEM = pl.BlockSpec(memory_space=pltpu.SMEM)
SCALE2 = HEAD_DIM ** (-0.5) * math.log2(math.e)


def call(kernel, out, operands, scratch=(), copies=1, cost=1, room=24):
    return pl.pallas_call(
        kernel,
        out_shape=[jax.ShapeDtypeStruct(x[1], x[2] if len(x) > 2 else BF16) for x in out],
        in_specs=[memory for memory, _ in operands],
        out_specs=[x[0] for x in out],
        scratch_shapes=[*scratch, pltpu.SemaphoreType.DMA((copies,))],
        compiler_params=pltpu.CompilerParams(vmem_limit_bytes=room * 2**20),
        cost_estimate=pl.CostEstimate(flops=cost, bytes_accessed=1, transcendentals=0),
    )(*(x for _, x in operands))


def start(sems, pairs, first=0):
    copies = [pltpu.make_async_copy(src, dst, sems.at[first + i]) for i, (src, dst) in enumerate(pairs)]
    for copy in copies:
        copy.start()
    return copies


def wait(copies):
    for copy in copies:
        copy.wait()


def dot_t(a, b):
    return lax.dot_general(a, b, (((1,), (1,)), ((), ())), preferred_element_type=F32)


def dot(a, b):
    return jnp.dot(a, b, preferred_element_type=F32)


def weigh(scores, valid):
    scores = jnp.where(valid, scores, NEG)
    peak = jnp.max(scores, axis=1, keepdims=True)
    weights = jnp.exp2((scores - peak) * SCALE2)
    return weights.astype(BF16), jnp.sum(weights, axis=1, keepdims=True), peak


def head(h):
    return slice(h * HEAD_DIM, (h + 1) * HEAD_DIM)


def pack_kernel(q_ref, k_ref, v_ref, w_ref, tail_ref, packed_ref, w_col_ref, tail, cols, w_col, sems):
    parts, count, per, _ = q_ref.shape
    near = pl.ds(count - SUMMARY // per, SUMMARY // per)
    come = []
    for i, ref in enumerate((k_ref, v_ref)):
        for f in range(2):
            come.append((ref.at[parts - 1, near, :, pl.ds((2 + f) * HEAD_DIM, HEAD_DIM)], tail.at[2 * i + f]))
    for i, ref in enumerate((q_ref, k_ref, v_ref)):
        come.append((ref.at[:, :, :, pl.ds(HEAD_DIM, HEAD_DIM)], cols.at[i]))
    quarter = HEAD_DIM // 4
    for i in range(4):
        come.append((w_ref.at[pl.ds(HEAD_DIM + i * quarter, quarter)], w_col.at[pl.ds(i * quarter, quarter)]))
    come = start(sems, come)
    first = len(come)
    wait(come[:4])
    gone = start(sems, [(tail, tail_ref)], first)
    for i, copy in enumerate(come[4:7]):
        wait([copy])
        pairs = [(cols.at[i, j], packed_ref.at[:, i, j]) for j in range(parts)]
        gone += start(sems, pairs, first + 1 + i * parts)
    for i, copy in enumerate(come[7:]):
        wait([copy])
        rows = pl.ds(i * quarter, quarter)
        gone += start(sems, [(w_col.at[rows], w_col_ref.at[rows])], first + 1 + 3 * parts + i)
    wait(gone)


def tail_kernel(k_ref, v_ref, tail, sems):
    block = k_ref.shape[0]
    pairs = []
    for i, ref in enumerate((k_ref, v_ref)):
        for f in range(2):
            pairs.append((ref.at[pl.ds(block - SUMMARY, SUMMARY), pl.ds((2 + f) * HEAD_DIM, HEAD_DIM)], tail.at[2 * i + f]))
    wait(start(sems, pairs))


def pack(queries, keys, values, out_weight, count, parts, per):
    width = queries.shape[1]
    tail_shape = (4, SUMMARY, HEAD_DIM)
    if per % 16:
        (tail,) = call(tail_kernel, [(VMEM, tail_shape)], [(HBM, keys), (HBM, values)], (), 4, room=63)
        cut = [x[:, HEAD_DIM : 2 * HEAD_DIM].reshape(parts, count, per, HEAD_DIM) for x in (queries, keys, values)]
        packed = jnp.stack(cut).transpose(2, 0, 1, 3, 4)
        return packed, tail, out_weight[HEAD_DIM : 2 * HEAD_DIM]
    tail_cut, w_shape = (4, SUMMARY // per, per, HEAD_DIM), (HEAD_DIM, out_weight.shape[1])
    tail, packed, w_col = call(
        pack_kernel,
        [(HBM, tail_cut), (HBM, (count, 3, parts, per, HEAD_DIM)), (HBM, w_shape)],
        [(HBM, x.reshape(parts, count, per, width)) for x in (queries, keys, values)] + [(HBM, out_weight)],
        [pltpu.VMEM(tail_cut, BF16), pltpu.VMEM((3, parts, count, per, HEAD_DIM), BF16), pltpu.VMEM(w_shape, BF16)],
        16 + 3 * parts,
        room=63,
    )
    return packed, tail.reshape(tail_shape), w_col


def column_kernel(columns, moved_ref, out_ref, held, sems):
    outer, _, inner, depth = moved_ref.shape
    rows = outer * inner
    copies = start(sems, [(moved_ref.at[:, i], held.at[i]) for i in range(3)])
    wait(copies[:2])
    q, k, v = (held.at[i] for i in range(3))
    step = HEAD_DIM
    starts = range(0, rows, step)
    at_k = lax.rem(lax.broadcasted_iota(jnp.int32, (1, rows), 1), columns)
    scores = []
    for first in starts:
        upto = first + step
        at_q = first + lax.broadcasted_iota(jnp.int32, (step, 1), 0)
        valid = (lax.rem(at_q, columns) == at_k[:, :upto]) & (lax.broadcasted_iota(jnp.int32, (1, upto), 1) <= at_q)
        scores.append(jnp.where(valid, dot_t(q[...].reshape(rows, depth)[first:upto], k[...].reshape(rows, depth)[:upto]), NEG))
    peaks = [jnp.max(x, axis=1, keepdims=True) for x in scores]
    weights = [jnp.exp2((x - y) * SCALE2).astype(BF16) for x, y in zip(scores, peaks)]
    wait(copies[2:])
    values = jnp.concatenate([v[...].reshape(rows, depth), jnp.ones((rows, depth), BF16)], axis=1)
    totals = [dot(x, values[: first + step]) for x, first in zip(weights, starts)]
    out = [x[:, :depth] / x[:, depth:] for x in totals]
    out_ref[...] = jnp.concatenate(out, axis=0).astype(BF16).reshape(outer, inner, depth)


def own_kernel(relative, q_ref, k_ref, v_ref, w_ref, lists_ref, slots_ref, row_ref, sum_ref, stat_ref, q_fixed, w_all, mult_ref, q_all, k_all, v_all, sems):
    pairs = [(q_ref, q_all), (k_ref, k_all), (v_ref, v_all)]
    pairs += [(q_ref.at[:, pl.ds(2 * HEAD_DIM, 2 * HEAD_DIM)], q_fixed)]
    pairs += [(w_ref.at[pl.ds(0, HEAD_DIM)], w_all.at[pl.ds(0, HEAD_DIM)])]
    pairs += [(w_ref.at[pl.ds(2 * HEAD_DIM, 2 * HEAD_DIM)], w_all.at[pl.ds(HEAD_DIM, 2 * HEAD_DIM)])]
    copies = start(sems, pairs)
    me = lax.axis_index("seq")
    tile = slots_ref[...] ^ me if relative else slots_ref[...]
    for f in range(2):
        times = sum((tile == lists_ref[f, i]).astype(F32) for i in range(lists_ref.shape[1]))
        mult_ref[f : f + 1, :] = jnp.where(tile < me, times, 0.0)
    wait(copies[:3])
    block, step = q_ref.shape[0], HEAD_DIM
    for first in range(0, block, step):
        upto = first + step
        rows = slice(first, upto)
        at_q = first + lax.broadcasted_iota(jnp.int32, (step, 1), 0)
        at_k = lax.broadcasted_iota(jnp.int32, (1, upto), 1)
        for h in (0, 2, 3):
            weights, denom, peak = weigh(dot_t(q_all[rows, head(h)], k_all[:upto, head(h)]), at_k <= at_q)
            total = dot(weights, v_all[:upto, head(h)])
            if h == 0:
                row_ref[rows] = (total / denom).astype(BF16)
            else:
                sum_ref[h - 2, rows] = total
                low = lax.broadcasted_iota(jnp.int32, (step, HEAD_DIM), 1) < HEAD_DIM // 2
                stat_ref[h - 2, rows] = jnp.where(low, denom, peak)
    wait(copies[3:])


def own_part(queries, keys, values, out_weight, lists, slots, relative):
    block = queries.shape[0]
    state = (VMEM, (2, block, HEAD_DIM), F32)
    weight_shape = (3 * HEAD_DIM, out_weight.shape[1])
    return call(
        functools.partial(own_kernel, relative),
        [(VMEM, (block, HEAD_DIM)), state, state, (VMEM, (block, 2 * HEAD_DIM)), (VMEM, weight_shape), (VMEM, (2, slots.shape[1]), F32)],
        [(HBM, x) for x in (queries, keys, values, out_weight)] + [(SMEM, lists), (VMEM, jnp.array(slots))],
        [pltpu.VMEM(queries.shape, BF16)] * 3,
        6,
        room=OWN_ROOM,
    )


def part_kernel(flips, parts, row_ref, sum_ref, stat_ref, q_ref, w_ref, mult_ref, *refs):
    tails, outs = refs[: -len(flips) - 1], refs[-len(flips) - 1 : -1]
    rows = q_ref.shape[0] // parts
    me = lax.axis_index("head")
    away_kv = [
        jnp.concatenate([x[:, i].reshape(x.shape[0] * SUMMARY, HEAD_DIM) for x in tails], axis=0) for i in range(4)
    ]
    here = [pl.ds(pl.multiple_of((me ^ flip) * rows, rows), rows) for flip in flips]
    items = [(at, f) for at in here for f in range(2)]
    mult = [mult_ref[f : f + 1, :] for f in range(2)]
    ones = jnp.ones_like(away_kv[0])
    values = [jnp.concatenate([away_kv[2 + f], ones], axis=1) for f in range(2)]
    away = [jnp.where(mult[f] > 0, dot_t(q_ref[at, head(f)], away_kv[f]), NEG) for at, f in items]
    own_peak = [stat_ref[f, at, HEAD_DIM // 2 : HEAD_DIM // 2 + 1] for at, f in items]
    peak = [jnp.maximum(x, jnp.max(y, axis=1, keepdims=True)) for x, y in zip(own_peak, away)]
    away = [(jnp.exp2((x - y) * SCALE2) * mult[f]).astype(BF16) for x, y, (_, f) in zip(away, peak, items)]
    total = [dot(x, values[f]) for x, (_, f) in zip(away, items)]
    shrink = [jnp.exp2((x - y) * SCALE2) for x, y in zip(own_peak, peak)]
    denom = [stat_ref[f, at, :1] * z + x[:, HEAD_DIM:] for (at, f), x, z in zip(items, total, shrink)]
    total = [sum_ref[f, at, :] * z + x[:, :HEAD_DIM] for (at, f), x, z in zip(items, total, shrink)]
    found = [(x / y).astype(BF16) for x, y in zip(total, denom)]
    for i, (at, out_ref) in enumerate(zip(here, outs)):
        out_ref[...] = dot(jnp.concatenate([row_ref[at, :], *found[2 * i : 2 * i + 2]], axis=1), w_ref[...]).astype(BF16)


def add_kernel(a_ref, b_ref, out_ref, done, sems):
    pieces = sems.shape[0]
    cut = done.shape[0] // pieces
    sent = []
    for i in range(pieces):
        rows = pl.ds(i * cut, cut)
        done[rows] = (a_ref[rows, :].astype(F32) + b_ref[rows, :].astype(F32)).astype(BF16)
        sent += start(sems, [(done.at[rows], out_ref.at[rows])], i)
    wait(sent)


def join_kernel(*refs):
    at = 0
    for ref in refs[:-2]:
        refs[-2][at : at + ref.shape[0]] = ref[...]
        at += ref.shape[0]


def last_kernel(own_ref, core_ref, far_ref, moved_ref, *refs):
    ws, (out_ref, moved, far, done, sems) = refs[:-6], refs[-5:]
    pieces = (sems.shape[0] - 1) // 2
    cut = done.shape[1] // pieces
    cols = [pl.ds(i * cut, cut) for i in range(pieces)]
    first, *copies = start(sems, [(moved_ref, moved)] + [(far_ref.at[:, c], far.at[:, c]) for c in cols])
    outer, heads, inner, depth = moved.shape
    me = lax.axis_index("head")
    wait([first])
    found = jnp.concatenate([moved[:, me ^ i].reshape(outer * inner, depth) for i in range(heads)], axis=1)
    sent = []
    for i, c in enumerate(cols):
        total = dot(found, jnp.concatenate([w[:, c] for w in ws], axis=0))
        total += own_ref[:, c].astype(F32) + core_ref[:, c].astype(F32)
        wait(copies[i : i + 1])
        done[:, c] = (total + far[:, c].astype(F32)).astype(BF16)
        sent += start(sems, [(done.at[:, c], out_ref.at[:, c])], 1 + pieces + i)
    wait(sent)


def settle_kernel(w_ref, out_ref, sems):
    wait(start(sems, [(w_ref.at[pl.ds(0, 16), pl.ds(0, HEAD_DIM)], out_ref)]))


def swap(x, axis, flip, count):
    return lax.ppermute(x, axis, [(i, i ^ flip) for i in range(count)])


def gather_tails(mine, count):
    bits = [(count // 4**i, 4) for i in range(1, 8) if count % 4**i == 0 and count // 4**i >= 2] + [(1, 2)]
    if count & (count - 1) or bits[-2:][0][0] != 2:
        return [lax.all_gather(mine, "seq")], None
    order, arrays = [0], [mine[None]]
    for step, radix in bits:
        if len(arrays) > 1:
            shape = (sum(x.shape[0] for x in arrays[1:]), *mine.shape)
            (came,) = call(join_kernel, [(VMEM, shape)], [(VMEM, x) for x in arrays[1:]], cost=JOIN_COST)
            arrays = list(lax.optimization_barrier((arrays[0], came)))
        if step == 1 or len(arrays) == 1:
            arrays += [swap(x, "seq", step * i, count) for i in range(1, radix) for x in arrays]
        else:
            held = jnp.concatenate(arrays, axis=0)
            arrays = [held] + [swap(held, "seq", step * i, count) for i in range(1, radix)]
        order = [j ^ (step * i) for i in range(radix) for j in order]
    return arrays, order


def per_device(queries, keys, values, summary_lists, out_weight):
    count, parts = lax.axis_size("seq"), lax.axis_size("head")
    block = queries.shape[0]
    me = lax.axis_index("seq")
    per = block // (count * parts)
    columns = per * parts

    packed, tail, w_col = pack(queries, keys, values, out_weight, count, parts, per)
    tails, order = gather_tails(tail, count)

    moved = lax.all_to_all(
        packed.reshape(count, 3 * columns, HEAD_DIM), "seq", split_axis=0, concat_axis=0, tiled=True
    )
    moved = moved.reshape(count, 3, columns, HEAD_DIM)
    if columns % 16:
        moved = moved.transpose(1, 0, 2, 3).reshape(1, 3, block, HEAD_DIM)

    held = [queries, keys, values, out_weight]
    if len(tails) > 1:
        *held, tails[0] = lax.optimization_barrier((*held, tails[0]))
    w_far = swap(w_col, "head", 2, parts)
    w_core = swap(w_col, "head", 1, parts)
    w_both = swap(w_far, "head", 1, parts)

    slots = np.repeat(np.arange(count) if order is None else np.array(order), SUMMARY)[None].astype(np.int32)
    shape = (block // parts, out_weight.shape[1])
    *own, mult = own_part(*held[:4], summary_lists[0], slots, order is not None)

    def partial_sums(flips):
        return call(
            functools.partial(part_kernel, flips, parts),
            [(VMEM, shape)] * len(flips),
            [(VMEM, x) for x in (*own, mult, *tails)],
        )

    both_sum, far_sum = partial_sums((3, 2))
    both_in = swap(both_sum, "head", 1, parts)
    (far_sum,) = call(add_kernel, [(HBM, shape)], [(VMEM, far_sum), (VMEM, both_in)], [pltpu.VMEM(shape, BF16)], 4)
    moved, _ = lax.optimization_barrier((moved, far_sum))
    column_shape = (moved.shape[0], moved.shape[2], HEAD_DIM)
    (column_out,) = call(
        functools.partial(column_kernel, columns),
        [(VMEM, column_shape)],
        [(HBM, moved)],
        [pltpu.VMEM((3, *column_shape), BF16)],
        3,
        COLUMN_COST,
    )

    far_in = swap(far_sum, "head", 2, parts)
    core_sum, own_sum = partial_sums((1, 0))
    core_in = swap(core_sum, "head", 1, parts)

    column_out = column_out.reshape(count * parts, per, HEAD_DIM)
    back = lax.all_to_all(column_out, ("seq", "head"), split_axis=0, concat_axis=0, tiled=True)
    back = back.reshape(count, parts, per, HEAD_DIM)
    if per % 16:
        back = back.transpose(1, 0, 2, 3).reshape(1, parts, count * per, HEAD_DIM)
    (settled,) = call(settle_kernel, [(VMEM, (16, HEAD_DIM))], [(HBM, w_both)], cost=SETTLE_COST)
    (mixed,) = call(
        last_kernel,
        [(HBM, shape)],
        [(VMEM, own_sum), (VMEM, core_in), (HBM, far_in), (HBM, back)] + [(VMEM, x) for x in (w_col, w_core, w_far, w_both, settled)],
        [pltpu.VMEM(back.shape, BF16), pltpu.VMEM(shape, BF16), pltpu.VMEM(shape, BF16)],
        1 + 2 * 1,
    )
    return mixed


def solution(mesh):
    return jax.shard_map(
        per_device,
        mesh=mesh,
        in_specs=(
            P("seq", "head"),
            P("seq", "head"),
            P("seq", "head"),
            P("seq", "head", None),
            P("head", None),
        ),
        out_specs=P(("seq", "head"), None),
        check_vma=False,
    )
```

```python
import functools
import math

import jax
import jax.numpy as jnp
import numpy as np
from jax import lax
from jax.experimental import pallas as pl
from jax.experimental.pallas import tpu as pltpu
from jax.sharding import PartitionSpec as P

HEAD_DIM = 128
SUMMARY = 32
NEG = -1e30
JOIN_COST = 10**9
COLUMN_COST = 10**9*3
OWN_ROOM = 48
SETTLE_COST = 25*10**8
BF16 = jnp.bfloat16
F32 = jnp.float32
HBM = pl.BlockSpec(memory_space=pltpu.HBM)
VMEM = pl.BlockSpec(memory_space=pltpu.VMEM)
SMEM = pl.BlockSpec(memory_space=pltpu.SMEM)
SCALE2 = HEAD_DIM ** (-0.5) * math.log2(math.e)


def call(kernel, out, operands, scratch=(), copies=1, cost=1, room=24):
    return pl.pallas_call(
        kernel,
        out_shape=[jax.ShapeDtypeStruct(x[1], x[2] if len(x) > 2 else BF16) for x in out],
        in_specs=[memory for memory, _ in operands],
        out_specs=[x[0] for x in out],
        scratch_shapes=[*scratch, pltpu.SemaphoreType.DMA((copies,))],
        compiler_params=pltpu.CompilerParams(vmem_limit_bytes=room * 2**20),
        cost_estimate=pl.CostEstimate(flops=cost, bytes_accessed=1, transcendentals=0),
    )(*(x for _, x in operands))


def start(sems, pairs, first=0):
    copies = [pltpu.make_async_copy(src, dst, sems.at[first + i]) for i, (src, dst) in enumerate(pairs)]
    for copy in copies:
        copy.start()
    return copies


def wait(copies):
    for copy in copies:
        copy.wait()


def dot_t(a, b):
    return lax.dot_general(a, b, (((1,), (1,)), ((), ())), preferred_element_type=F32)


def dot(a, b):
    return jnp.dot(a, b, preferred_element_type=F32)


def weigh(scores, valid):
    scores = jnp.where(valid, scores, NEG)
    peak = jnp.max(scores, axis=1, keepdims=True)
    weights = jnp.exp2((scores - peak) * SCALE2)
    return weights.astype(BF16), jnp.sum(weights, axis=1, keepdims=True), peak


def head(h):
    return slice(h * HEAD_DIM, (h + 1) * HEAD_DIM)


def pack_kernel(q_ref, k_ref, v_ref, w_ref, tail_ref, packed_ref, w_col_ref, tail, cols, w_col, sems):
    parts, count, per, _ = q_ref.shape
    near = pl.ds(count - SUMMARY // per, SUMMARY // per)
    come = []
    for i, ref in enumerate((k_ref, v_ref)):
        for f in range(2):
            come.append((ref.at[parts - 1, near, :, pl.ds((2 + f) * HEAD_DIM, HEAD_DIM)], tail.at[2 * i + f]))
    for i, ref in enumerate((q_ref, k_ref, v_ref)):
        come.append((ref.at[:, :, :, pl.ds(HEAD_DIM, HEAD_DIM)], cols.at[i]))
    quarter = HEAD_DIM // 4
    for i in range(4):
        come.append((w_ref.at[pl.ds(HEAD_DIM + i * quarter, quarter)], w_col.at[pl.ds(i * quarter, quarter)]))
    come = start(sems, come)
    first = len(come)
    wait(come[:4])
    gone = start(sems, [(tail, tail_ref)], first)
    for i, copy in enumerate(come[4:7]):
        wait([copy])
        pairs = [(cols.at[i, j], packed_ref.at[:, i, j]) for j in range(parts)]
        gone += start(sems, pairs, first + 1 + i * parts)
    for i, copy in enumerate(come[7:]):
        wait([copy])
        rows = pl.ds(i * quarter, quarter)
        gone += start(sems, [(w_col.at[rows], w_col_ref.at[rows])], first + 1 + 3 * parts + i)
    wait(gone)


def tail_kernel(k_ref, v_ref, tail, sems):
    block = k_ref.shape[0]
    pairs = []
    for i, ref in enumerate((k_ref, v_ref)):
        for f in range(2):
            pairs.append((ref.at[pl.ds(block - SUMMARY, SUMMARY), pl.ds((2 + f) * HEAD_DIM, HEAD_DIM)], tail.at[2 * i + f]))
    wait(start(sems, pairs))


def pack(queries, keys, values, out_weight, count, parts, per):
    width = queries.shape[1]
    tail_shape = (4, SUMMARY, HEAD_DIM)
    if per % 16:
        (tail,) = call(tail_kernel, [(VMEM, tail_shape)], [(HBM, keys), (HBM, values)], (), 4, room=63)
        cut = [x[:, HEAD_DIM : 2 * HEAD_DIM].reshape(parts, count, per, HEAD_DIM) for x in (queries, keys, values)]
        packed = jnp.stack(cut).transpose(2, 0, 1, 3, 4)
        return packed, tail, out_weight[HEAD_DIM : 2 * HEAD_DIM]
    tail_cut, w_shape = (4, SUMMARY // per, per, HEAD_DIM), (HEAD_DIM, out_weight.shape[1])
    tail, packed, w_col = call(
        pack_kernel,
        [(HBM, tail_cut), (HBM, (count, 3, parts, per, HEAD_DIM)), (HBM, w_shape)],
        [(HBM, x.reshape(parts, count, per, width)) for x in (queries, keys, values)] + [(HBM, out_weight)],
        [pltpu.VMEM(tail_cut, BF16), pltpu.VMEM((3, parts, count, per, HEAD_DIM), BF16), pltpu.VMEM(w_shape, BF16)],
        16 + 3 * parts,
        room=63,
    )
    return packed, tail.reshape(tail_shape), w_col


def column_kernel(columns, moved_ref, out_ref, held, sems):
    outer, _, inner, depth = moved_ref.shape
    rows = outer * inner
    copies = start(sems, [(moved_ref.at[:, i], held.at[i]) for i in range(3)])
    wait(copies[:2])
    q, k, v = (held.at[i] for i in range(3))
    step = HEAD_DIM
    starts = range(0, rows, step)
    at_k = lax.rem(lax.broadcasted_iota(jnp.int32, (1, rows), 1), columns)
    scores = []
    for first in starts:
        upto = first + step
        at_q = first + lax.broadcasted_iota(jnp.int32, (step, 1), 0)
        valid = (lax.rem(at_q, columns) == at_k[:, :upto]) & (lax.broadcasted_iota(jnp.int32, (1, upto), 1) <= at_q)
        scores.append(jnp.where(valid, dot_t(q[...].reshape(rows, depth)[first:upto], k[...].reshape(rows, depth)[:upto]), NEG))
    peaks = [jnp.max(x, axis=1, keepdims=True) for x in scores]
    weights = [jnp.exp2((x - y) * SCALE2).astype(BF16) for x, y in zip(scores, peaks)]
    wait(copies[2:])
    values = jnp.concatenate([v[...].reshape(rows, depth), jnp.ones((rows, depth), BF16)], axis=1)
    totals = [dot(x, values[: first + step]) for x, first in zip(weights, starts)]
    out = [x[:, :depth] / x[:, depth:] for x in totals]
    out_ref[...] = jnp.concatenate(out, axis=0).astype(BF16).reshape(outer, inner, depth)


def own_kernel(relative, q_ref, k_ref, v_ref, w_ref, lists_ref, slots_ref, row_ref, sum_ref, stat_ref, q_fixed, w_all, mult_ref, q_all, k_all, v_all, sems):
    pairs = [(q_ref, q_all), (k_ref, k_all), (v_ref, v_all)]
    pairs += [(q_ref.at[:, pl.ds(2 * HEAD_DIM, 2 * HEAD_DIM)], q_fixed)]
    pairs += [(w_ref.at[pl.ds(0, HEAD_DIM)], w_all.at[pl.ds(0, HEAD_DIM)])]
    pairs += [(w_ref.at[pl.ds(2 * HEAD_DIM, 2 * HEAD_DIM)], w_all.at[pl.ds(HEAD_DIM, 2 * HEAD_DIM)])]
    copies = start(sems, pairs)
    me = lax.axis_index("seq")
    tile = slots_ref[...] ^ me if relative else slots_ref[...]
    for f in range(2):
        times = sum((tile == lists_ref[f, i]).astype(F32) for i in range(lists_ref.shape[1]))
        mult_ref[f : f + 1, :] = jnp.where(tile < me, times, 0.0)
    wait(copies[:3])
    block, step = q_ref.shape[0], HEAD_DIM
    for first in range(0, block, step):
        upto = first + step
        rows = slice(first, upto)
        at_q = first + lax.broadcasted_iota(jnp.int32, (step, 1), 0)
        at_k = lax.broadcasted_iota(jnp.int32, (1, upto), 1)
        for h in (0, 2, 3):
            weights, denom, peak = weigh(dot_t(q_all[rows, head(h)], k_all[:upto, head(h)]), at_k <= at_q)
            total = dot(weights, v_all[:upto, head(h)])
            if h == 0:
                row_ref[rows] = (total / denom).astype(BF16)
            else:
                sum_ref[h - 2, rows] = total
                low = lax.broadcasted_iota(jnp.int32, (step, HEAD_DIM), 1) < HEAD_DIM // 2
                stat_ref[h - 2, rows] = jnp.where(low, denom, peak)
    wait(copies[3:])


def own_part(queries, keys, values, out_weight, lists, slots, relative):
    block = queries.shape[0]
    state = (VMEM, (2, block, HEAD_DIM), F32)
    weight_shape = (3 * HEAD_DIM, out_weight.shape[1])
    return call(
        functools.partial(own_kernel, relative),
        [(VMEM, (block, HEAD_DIM)), state, state, (VMEM, (block, 2 * HEAD_DIM)), (VMEM, weight_shape), (VMEM, (2, slots.shape[1]), F32)],
        [(HBM, x) for x in (queries, keys, values, out_weight)] + [(SMEM, lists), (VMEM, jnp.array(slots))],
        [pltpu.VMEM(queries.shape, BF16)] * 3,
        6,
        room=OWN_ROOM,
    )


def part_kernel(flips, parts, row_ref, sum_ref, stat_ref, q_ref, w_ref, mult_ref, *refs):
    tails, outs = refs[: -len(flips) - 1], refs[-len(flips) - 1 : -1]
    rows = q_ref.shape[0] // parts
    me = lax.axis_index("head")
    away_kv = [
        jnp.concatenate([x[:, i].reshape(x.shape[0] * SUMMARY, HEAD_DIM) for x in tails], axis=0) for i in range(4)
    ]
    here = [pl.ds(pl.multiple_of((me ^ flip) * rows, rows), rows) for flip in flips]
    items = [(at, f) for at in here for f in range(2)]
    mult = [mult_ref[f : f + 1, :] for f in range(2)]
    ones = jnp.ones_like(away_kv[0])
    values = [jnp.concatenate([away_kv[2 + f], ones], axis=1) for f in range(2)]
    away = [jnp.where(mult[f] > 0, dot_t(q_ref[at, head(f)], away_kv[f]), NEG) for at, f in items]
    own_peak = [stat_ref[f, at, HEAD_DIM // 2 : HEAD_DIM // 2 + 1] for at, f in items]
    peak = [jnp.maximum(x, jnp.max(y, axis=1, keepdims=True)) for x, y in zip(own_peak, away)]
    away = [(jnp.exp2((x - y) * SCALE2) * mult[f]).astype(BF16) for x, y, (_, f) in zip(away, peak, items)]
    total = [dot(x, values[f]) for x, (_, f) in zip(away, items)]
    shrink = [jnp.exp2((x - y) * SCALE2) for x, y in zip(own_peak, peak)]
    denom = [stat_ref[f, at, :1] * z + x[:, HEAD_DIM:] for (at, f), x, z in zip(items, total, shrink)]
    total = [sum_ref[f, at, :] * z + x[:, :HEAD_DIM] for (at, f), x, z in zip(items, total, shrink)]
    found = [(x / y).astype(BF16) for x, y in zip(total, denom)]
    for i, (at, out_ref) in enumerate(zip(here, outs)):
        out_ref[...] = dot(jnp.concatenate([row_ref[at, :], *found[2 * i : 2 * i + 2]], axis=1), w_ref[...]).astype(BF16)


def add_kernel(a_ref, b_ref, out_ref, done, sems):
    pieces = sems.shape[0]
    cut = done.shape[0] // pieces
    sent = []
    for i in range(pieces):
        rows = pl.ds(i * cut, cut)
        done[rows] = (a_ref[rows, :].astype(F32) + b_ref[rows, :].astype(F32)).astype(BF16)
        sent += start(sems, [(done.at[rows], out_ref.at[rows])], i)
    wait(sent)


def join_kernel(*refs):
    at = 0
    for ref in refs[:-2]:
        refs[-2][at : at + ref.shape[0]] = ref[...]
        at += ref.shape[0]


def last_kernel(own_ref, core_ref, far_ref, moved_ref, *refs):
    ws, (out_ref, moved, far, done, sems) = refs[:-6], refs[-5:]
    pieces = (sems.shape[0] - 1) // 2
    cut = done.shape[1] // pieces
    cols = [pl.ds(i * cut, cut) for i in range(pieces)]
    *copies, first = start(sems, [(far_ref.at[:, c], far.at[:, c]) for c in cols] + [(moved_ref, moved)])
    outer, heads, inner, depth = moved.shape
    me = lax.axis_index("head")
    wait([first])
    found = jnp.concatenate([moved[:, me ^ i].reshape(outer * inner, depth) for i in range(heads)], axis=1)
    sent = []
    for i, c in enumerate(cols):
        total = dot(found, jnp.concatenate([w[:, c] for w in ws], axis=0))
        total += own_ref[:, c].astype(F32) + core_ref[:, c].astype(F32)
        wait(copies[i : i + 1])
        done[:, c] = (total + far[:, c].astype(F32)).astype(BF16)
        sent += start(sems, [(done.at[:, c], out_ref.at[:, c])], 1 + pieces + i)
    wait(sent)


def settle_kernel(w_ref, out_ref, sems):
    wait(start(sems, [(w_ref.at[pl.ds(0, 16), pl.ds(0, HEAD_DIM)], out_ref)]))


def swap(x, axis, flip, count):
    return lax.ppermute(x, axis, [(i, i ^ flip) for i in range(count)])


def gather_tails(mine, count):
    bits = [(count // 4**i, 4) for i in range(1, 8) if count % 4**i == 0 and count // 4**i >= 2] + [(1, 2)]
    if count & (count - 1) or bits[-2:][0][0] != 2:
        return [lax.all_gather(mine, "seq")], None
    order, arrays = [0], [mine[None]]
    for step, radix in bits:
        if len(arrays) > 1:
            shape = (sum(x.shape[0] for x in arrays[1:]), *mine.shape)
            (came,) = call(join_kernel, [(VMEM, shape)], [(VMEM, x) for x in arrays[1:]], cost=JOIN_COST)
            arrays = list(lax.optimization_barrier((arrays[0], came)))
        if step == 1 or len(arrays) == 1:
            arrays += [swap(x, "seq", step * i, count) for i in range(1, radix) for x in arrays]
        else:
            held = jnp.concatenate(arrays, axis=0)
            arrays = [held] + [swap(held, "seq", step * i, count) for i in range(1, radix)]
        order = [j ^ (step * i) for i in range(radix) for j in order]
    return arrays, order


def per_device(queries, keys, values, summary_lists, out_weight):
    count, parts = lax.axis_size("seq"), lax.axis_size("head")
    block = queries.shape[0]
    me = lax.axis_index("seq")
    per = block // (count * parts)
    columns = per * parts

    packed, tail, w_col = pack(queries, keys, values, out_weight, count, parts, per)
    tails, order = gather_tails(tail, count)

    moved = lax.all_to_all(
        packed.reshape(count, 3 * columns, HEAD_DIM), "seq", split_axis=0, concat_axis=0, tiled=True
    )
    moved = moved.reshape(count, 3, columns, HEAD_DIM)
    if columns % 16:
        moved = moved.transpose(1, 0, 2, 3).reshape(1, 3, block, HEAD_DIM)

    held = [queries, keys, values, out_weight]
    if len(tails) > 1:
        *held, tails[0] = lax.optimization_barrier((*held, tails[0]))
    w_far = swap(w_col, "head", 2, parts)
    w_core = swap(w_col, "head", 1, parts)
    w_both = swap(w_far, "head", 1, parts)

    slots = np.repeat(np.arange(count) if order is None else np.array(order), SUMMARY)[None].astype(np.int32)
    shape = (block // parts, out_weight.shape[1])
    *own, mult = own_part(*held[:4], summary_lists[0], slots, order is not None)

    def partial_sums(flips):
        return call(
            functools.partial(part_kernel, flips, parts),
            [(VMEM, shape)] * len(flips),
            [(VMEM, x) for x in (*own, mult, *tails)],
        )

    both_sum, far_sum = partial_sums((3, 2))
    both_in = swap(both_sum, "head", 1, parts)
    (far_sum,) = call(add_kernel, [(HBM, shape)], [(VMEM, far_sum), (VMEM, both_in)], [pltpu.VMEM(shape, BF16)], 4)
    moved, _ = lax.optimization_barrier((moved, far_sum))
    column_shape = (moved.shape[0], moved.shape[2], HEAD_DIM)
    (column_out,) = call(
        functools.partial(column_kernel, columns),
        [(VMEM, column_shape)],
        [(HBM, moved)],
        [pltpu.VMEM((3, *column_shape), BF16)],
        3,
        COLUMN_COST,
    )

    far_in = swap(far_sum, "head", 2, parts)
    core_sum, own_sum = partial_sums((1, 0))
    core_in = swap(core_sum, "head", 1, parts)

    column_out = column_out.reshape(count * parts, per, HEAD_DIM)
    back = lax.all_to_all(column_out, ("seq", "head"), split_axis=0, concat_axis=0, tiled=True)
    back = back.reshape(count, parts, per, HEAD_DIM)
    if per % 16:
        back = back.transpose(1, 0, 2, 3).reshape(1, parts, count * per, HEAD_DIM)
    (settled,) = call(settle_kernel, [(VMEM, (16, HEAD_DIM))], [(HBM, w_both)], cost=SETTLE_COST)
    (mixed,) = call(
        last_kernel,
        [(HBM, shape)],
        [(VMEM, own_sum), (VMEM, core_in), (HBM, far_in), (HBM, back)] + [(VMEM, x) for x in (w_col, w_core, w_far, w_both, settled)],
        [pltpu.VMEM(back.shape, BF16), pltpu.VMEM(shape, BF16), pltpu.VMEM(shape, BF16)],
        1 + 2 * 1,
    )
    return mixed


def solution(mesh):
    return jax.shard_map(
        per_device,
        mesh=mesh,
        in_specs=(
            P("seq", "head"),
            P("seq", "head"),
            P("seq", "head"),
            P("seq", "head", None),
            P("head", None),
        ),
        out_specs=P(("seq", "head"), None),
        check_vma=False,
    )
```
